32 devices in a mesh: grp: 2 (over y), ep: 16 (over z, x, core), tp: 1.
Axes of the slice: x: 2, y: 2, z: 4, core: 2. Of those that a mesh axis runs over, the one named last changes fastest.
Arguments:
- tokens: bfloat16 [2048, 3584], P(('grp', 'ep'), 'tp'), parts along dimension 0, may hold values from -6 to 6
- gate_scores: float32 [2048, 8], P(('grp', 'ep')), parts along dimension 0, may hold values from 0.05 to 1
- route_ids: int32 [2048, 8], P(('grp', 'ep')), parts along dimension 0, may hold values from 0 to 15, all different within a row; in each aligned block of 64 rows (0 to 63, 64 to 127, ...) at most 40 rows name the same one
- gate_codes: float32 [16, 896, 1024], P('ep', None, 'tp'), may hold values from 0 to 65535, as said below
- up_codes: float32 [16, 896, 1024], P('ep', None, 'tp'), may hold values from 0 to 65535, as said below
- down_codes: float32 [16, 256, 3584], P('ep', None, 'tp'), may hold values from 0 to 65535, as said below
- gate_scale: bfloat16 [16, 28, 1024], P('ep', None, 'tp'), may hold values from 0.0019989014 to 0.007507324
- up_scale: bfloat16 [16, 28, 1024], P('ep', None, 'tp'), may hold values from 0.0019989014 to 0.007507324
- down_scale: bfloat16 [16, 8, 3584], P('ep', None, 'tp'), may hold values from 0.0037384033 to 0.014038086
- gate_zero: bfloat16 [16, 28, 1024], P('ep', None, 'tp'), may hold values from 6 to 9
- up_zero: bfloat16 [16, 28, 1024], P('ep', None, 'tp'), may hold values from 6 to 9
- down_zero: bfloat16 [16, 8, 3584], P('ep', None, 'tp'), may hold values from 6 to 9
Outputs:
- mixed: bfloat16 [2048, 3584], P(('grp', 'ep'), 'tp'), parts along dimension 0
The draws below stay inside these ranges and needn't reach their ends.
There are 2 independent parts, one for each index of `grp`. The reference program is written for one: setup_inputs(seed, part) draws one part's arguments, and reference() takes and returns one part's arrays. A program takes and returns all parts, laid end to end along the dimension named above; an argument that names none is the same for every part. Nothing has to cross between parts.
Inputs may be any that keep to these rules, and one draw needn't show every extreme that they name: `route_ids`: each row names 8 different experts; within each aligned block of 64 rows no expert is named by more than 40 rows, a bound that some block reaches. `gate_codes`: every entry is a whole number. `up_codes`: every entry is a whole number. `down_codes`: every entry is a whole number.
All inputs are finite; a program needn't handle non-finite values.
Results may differ from the reference program's by a relative error of at most 0.0076.
Values may be sent and summed in bfloat16 or wider, within the bound.
No kernel may reach another device: no remote copies, remote signals or barrier semaphores. Data moves between devices by JAX's collectives and lax.ppermute only.
A program may use at most 192 MiB of HBM per device.

```python
import math
import jax
import jax.numpy as jnp
import numpy as np
from jax import lax

D = 3584
FF = 1024
TOPK = 8
TOK_DEV = 64
EXPERTS = 16
CAP = 40
TOKENS = 1024
N_EP = 16


def draw_gate_codes(key, part):
    key = jax.random.fold_in(key, 21)
    return jax.random.randint(key, (EXPERTS, D // 4, FF), 0, 65536, dtype=jnp.int32).astype(jnp.float32)


def draw_up_codes(key, part):
    key = jax.random.fold_in(key, 22)
    return jax.random.randint(key, (EXPERTS, D // 4, FF), 0, 65536, dtype=jnp.int32).astype(jnp.float32)


def draw_down_codes(key, part):
    key = jax.random.fold_in(key, 23)
    return jax.random.randint(key, (EXPERTS, FF // 4, D), 0, 65536, dtype=jnp.int32).astype(jnp.float32)


def steps_of(own_key, dims, split, least, top_value):
    def one(axis_at, parts):
        heights = jax.random.uniform(jax.random.fold_in(jax.random.fold_in(own_key, 6), axis_at), (parts,), jnp.float32, least / len(split), top_value / len(split))
        return jnp.repeat(jnp.exp(heights), dims[axis_at] // parts).reshape((-1,) + (1,) * (len(dims) - axis_at - 1))

    factor_of = one(*split[0])
    for cut in split[1:]:
        factor_of = factor_of * one(*cut)
    return factor_of


def deal_out(key, own, number, rows, number_of, top, most, skew):
    sequence = jax.random.permutation(key, number_of)
    crowded, ordinary = portions_of(number_of, rows * top, most, skew, True), portions_of(number_of, rows * top, most, skew, False)
    places = jnp.arange(number_of)

    def named(lengths, rotation):
        used = int((lengths > 0).sum())
        fixed = max(1, used // 4)
        shifted = fixed + (places - fixed + rotation * (used - fixed)) % max(1, number_of - fixed)
        return jnp.zeros((number_of,), jnp.int32).at[sequence[jnp.where(places < fixed, places, shifted)]].set(jnp.asarray(lengths, jnp.int32))

    lengths = jnp.where(number % 4 == 0, named(crowded, number // 4), named(ordinary, number - number // 4 - 1))
    mixed = jax.random.permutation(jax.random.fold_in(own, 3), number_of)
    giver, receiver = mixed[0:number_of // 2 * 2:2], mixed[1:number_of // 2 * 2:2]
    slack = jnp.minimum(lengths[giver] - 1, most - lengths[receiver]) // 2
    slack = jnp.where((giver == sequence[0]) | (receiver == sequence[0]) | (lengths[receiver] == 0), 0, jnp.maximum(slack, 0))
    shifted = jax.random.randint(jax.random.fold_in(own, 4), (number_of // 2,), 0, 1 << 20) % (slack + 1)
    lengths = lengths.at[giver].add(-shifted).at[receiver].add(shifted)
    members = jnp.searchsorted(jnp.cumsum(lengths), jnp.arange(rows * top), side="right").astype(jnp.int32)
    listing = members.reshape(top, rows).T
    listing = listing[jax.random.permutation(jax.random.fold_in(own, 1), rows)]
    rotation = jax.random.randint(jax.random.fold_in(own, 2), (rows, 1), 0, top)
    return jnp.take_along_axis(listing, (jnp.arange(top)[None, :] + rotation) % top, axis=1)


def portions_of(count, total, most, skew, full):
    portions = [(1 << 20) // math.isqrt(grade ** skew) + 1 for grade in range(1, count + 1)]
    largest = most if full else min(most, max(-(-total // count), total * portions[0] // sum(portions)))
    least = 1 if total - largest >= count - 1 else 0
    given, surplus = [largest] + [least] * (count - 1), total - largest - least * (count - 1)
    while surplus > 0:
        movable = [i for i in range(1, count) if given[i] < largest] or [i for i in range(1, count) if given[i] < most]
        whole, left = sum([portions[i] for i in movable]), surplus
        for i in movable:
            more = min(most - given[i], max(1, left * portions[i] // whole), surplus)
            given[i] = given[i] + more
            surplus = surplus - more
    return np.array(given)


def bell_draw(rng, shape, scale, bound, shards=(), kind=jnp.bfloat16):
    entries = jax.random.normal(rng, shape, jnp.float32) * scale
    if len(shards) > 0:
        entries = steps_of(rng, shape, shards, -0.22, 0.18) * entries
    return jnp.clip(entries, min=-bound, max=bound).astype(kind)


def setup_inputs(seed: int = 0, part: int = 0) -> dict:
    splits = jax.random.split(jax.random.key(seed), 13)
    part_splits = jax.random.split(jax.random.fold_in(splits[12], part), 13)
    tokens = bell_draw(part_splits[0], (TOKENS, D), 1.0, 6.0, ((0, 16),))
    gate_scores = jnp.clip(0.05 + 0.95 * jax.random.uniform(part_splits[1], (TOKENS, TOPK), jnp.float32) ** steps_of(part_splits[1], (TOKENS, TOPK), ((0, 16),), -0.2, 0.2), 0.05, 1.0)
    route_ids_keys = jax.random.split(jax.random.fold_in(part_splits[2], 1), TOKENS // TOK_DEV)
    route_ids_turns = jax.random.permutation(jax.random.fold_in(part_splits[2], 3), TOKENS // TOK_DEV)
    route_ids = jax.vmap(lambda own, number: deal_out(jax.random.fold_in(part_splits[2], 2), own, number, TOK_DEV, EXPERTS, TOPK, CAP, 2))(route_ids_keys, route_ids_turns).reshape((TOKENS, TOPK))
    gate_codes = draw_gate_codes(jax.random.fold_in(splits[12], 71), part)
    up_codes = draw_up_codes(jax.random.fold_in(splits[12], 71), part)
    down_codes = draw_down_codes(jax.random.fold_in(splits[12], 71), part)
    gate_scale = jnp.clip(jnp.exp(math.log(0.007507324) - 1.3232814 * jax.random.uniform(splits[6], (EXPERTS, D // 128, FF), jnp.float32) ** steps_of(splits[6], (EXPERTS, D // 128, FF), ((0, 16),), -0.2, 0.2)), 0.0019989014, 0.007507324).astype(jnp.bfloat16)
    up_scale = jnp.clip(jnp.exp(math.log(0.007507324) - 1.3232814 * jax.random.uniform(splits[7], (EXPERTS, D // 128, FF), jnp.float32) ** steps_of(splits[7], (EXPERTS, D // 128, FF), ((0, 16),), -0.2, 0.2)), 0.0019989014, 0.007507324).astype(jnp.bfloat16)
    down_scale = jnp.clip(jnp.exp(math.log(0.014038086) - 1.3231155 * jax.random.uniform(splits[8], (EXPERTS, FF // 128, D), jnp.float32) ** steps_of(splits[8], (EXPERTS, FF // 128, D), ((0, 16),), -0.2, 0.2)), 0.0037384033, 0.014038086).astype(jnp.bfloat16)
    gate_zero = jnp.clip(6.0 + 3.0 * jax.random.uniform(splits[9], (EXPERTS, D // 128, FF), jnp.float32) ** steps_of(splits[9], (EXPERTS, D // 128, FF), ((0, 16),), -0.2, 0.2), 6.0, 9.0).astype(jnp.bfloat16)
    up_zero = jnp.clip(6.0 + 3.0 * jax.random.uniform(splits[10], (EXPERTS, D // 128, FF), jnp.float32) ** steps_of(splits[10], (EXPERTS, D // 128, FF), ((0, 16),), -0.2, 0.2), 6.0, 9.0).astype(jnp.bfloat16)
    down_zero = jnp.clip(6.0 + 3.0 * jax.random.uniform(splits[11], (EXPERTS, FF // 128, D), jnp.float32) ** steps_of(splits[11], (EXPERTS, FF // 128, D), ((0, 16),), -0.2, 0.2), 6.0, 9.0).astype(jnp.bfloat16)
    return {"tokens": tokens, "gate_scores": gate_scores, "route_ids": route_ids, "gate_codes": gate_codes, "up_codes": up_codes, "down_codes": down_codes, "gate_scale": gate_scale, "up_scale": up_scale, "down_scale": down_scale, "gate_zero": gate_zero, "up_zero": up_zero, "down_zero": down_zero}


route_scale = 2.5


def dequantize(words, scales, zeros):
    groups = scales.shape[0]
    packed = words.astype(jnp.float32).reshape(groups, words.shape[0] // groups, 1, words.shape[1])
    powers = jnp.array([1.0, 16.0, 256.0, 4096.0], jnp.float32)[None, None, :, None]
    lower = jnp.floor(packed / powers)
    higher = jnp.floor(packed / (16.0 * powers))
    codes = lower - 16.0 * higher
    values = (codes - zeros.astype(jnp.float32)[:, None, None, :]) * scales.astype(jnp.float32)[:, None, None, :]
    return values.reshape(-1, words.shape[1]).astype(jnp.bfloat16)


def reference(tokens, gate_scores, route_ids, gate_codes, up_codes, down_codes, gate_scale, up_scale, down_scale, gate_zero, up_zero, down_zero):
    flat_ids = route_ids.reshape(-1).astype(jnp.int32)
    total = flat_ids.shape[0]
    order = jnp.argsort(flat_ids, stable=True).astype(jnp.int32)
    sorted_ids = flat_ids[order]
    starts = jnp.searchsorted(sorted_ids, jnp.arange(EXPERTS, dtype=jnp.int32)).astype(jnp.int32)
    ends = jnp.concatenate([starts[1:], jnp.full((1,), total, jnp.int32)]).astype(jnp.int32)
    rows = N_EP * CAP
    token_of = jnp.concatenate([(order // TOPK).astype(jnp.int32), jnp.zeros((rows,), jnp.int32)])

    def one_expert(expert):
        begin = starts[expert].astype(jnp.int32)
        picked = lax.dynamic_slice_in_dim(token_of, begin, rows)
        live = jnp.arange(rows, dtype=jnp.int32) < (ends[expert] - begin)
        inputs = tokens[picked]
        w_gate = dequantize(gate_codes[expert], gate_scale[expert], gate_zero[expert])
        w_up = dequantize(up_codes[expert], up_scale[expert], up_zero[expert])
        w_down = dequantize(down_codes[expert], down_scale[expert], down_zero[expert])
        gate = jnp.dot(inputs, w_gate, preferred_element_type=jnp.float32)
        up = jnp.dot(inputs, w_up, preferred_element_type=jnp.float32)
        hidden = (jax.nn.silu(gate) * up).astype(jnp.bfloat16)
        answer = jnp.dot(hidden, w_down, preferred_element_type=jnp.float32).astype(jnp.bfloat16)
        return jnp.where(live[:, None], answer, jnp.zeros_like(answer))

    outputs = lax.map(one_expert, jnp.arange(EXPERTS, dtype=jnp.int32))
    inverse = jnp.zeros((total,), jnp.int32).at[order].set(jnp.arange(total, dtype=jnp.int32))
    position = flat_ids * rows + inverse - starts[flat_ids]
    chosen = outputs.reshape(-1, outputs.shape[-1])[position].astype(jnp.float32)
    chosen = chosen.reshape(route_ids.shape[0], route_ids.shape[1], -1)
    weights = route_scale * gate_scores / jnp.sum(gate_scores, axis=1, keepdims=True)
    return jnp.sum(weights[:, :, None] * chosen, axis=1).astype(jnp.bfloat16)
```

```python
import functools

import jax
import jax.numpy as jnp
from jax import lax
from jax.experimental import pallas as pl
from jax.experimental.pallas import tpu as pltpu
from jax.sharding import PartitionSpec as P

route_scale = 2.5
GROUP = 128
WORD = 4
CHUNK = GROUP * WORD
EXTRA = 128
F32 = jnp.float32
BF16 = jnp.bfloat16


def dequantize(words, scales, zeros):
    groups = scales.shape[0]
    packed = words.reshape(groups, words.shape[0] // groups, 1, words.shape[1])
    powers = jnp.array([1.0, 16.0, 256.0, 4096.0], jnp.float32)[None, None, :, None]
    lower = jnp.floor(packed / powers)
    higher = jnp.floor(packed / (16.0 * powers))
    codes = lower - 16.0 * higher
    values = (codes - zeros.astype(jnp.float32)[:, None, None, :]) * scales.astype(jnp.float32)[
        :, None, None, :
    ]
    return values.reshape(-1, words.shape[1]).astype(jnp.bfloat16)


def routed(
    tokens,
    gate_scores,
    route_ids,
    gate_codes,
    up_codes,
    down_codes,
    gate_scale,
    up_scale,
    down_scale,
    gate_zero,
    up_zero,
    down_zero,
):
    experts = lax.axis_size("ep")
    tok_rows, half_width = tokens.shape
    topk = route_ids.shape[1]
    capacity = min(tok_rows, max(2, 5 * tok_rows * topk // (4 * experts)))
    w_gate = dequantize(gate_codes[0], gate_scale[0], gate_zero[0])
    w_up = dequantize(up_codes[0], up_scale[0], up_zero[0])
    w_down = dequantize(down_codes[0], down_scale[0], down_zero[0])
    flat_ids = route_ids.reshape(-1)
    onehot = (flat_ids[:, None] == jnp.arange(experts, dtype=jnp.int32)[None, :]).astype(jnp.int32)
    earlier = jnp.cumsum(onehot, axis=0) - onehot
    slot = jnp.sum(earlier * onehot, axis=1)
    target = (flat_ids * capacity + slot).reshape(tok_rows, topk)
    places = jnp.arange(experts * capacity, dtype=jnp.int32)
    selector = jnp.sum(
        (places[:, None, None] == target[None, :, :]).astype(jnp.float32), axis=2
    ).astype(jnp.bfloat16)
    outgoing = jnp.dot(selector, tokens, preferred_element_type=jnp.float32).astype(jnp.bfloat16)
    outgoing = outgoing.reshape(experts, capacity, half_width)
    whole = lax.all_gather(
        lax.all_to_all(outgoing, "ep", split_axis=0, concat_axis=0, tiled=True),
        "tp",
        axis=2,
        tiled=True,
    )
    count = whole.shape[1]
    flat_rows = whole.reshape(-1, whole.shape[2])
    gate = jnp.dot(flat_rows, w_gate, preferred_element_type=jnp.float32)
    up = jnp.dot(flat_rows, w_up, preferred_element_type=jnp.float32)
    hidden = (jax.nn.silu(gate) * up).astype(jnp.bfloat16)
    summed = jnp.dot(
        lax.all_gather(hidden, "tp", axis=1, tiled=True), w_down, preferred_element_type=jnp.float32
    )
    answer = summed.astype(jnp.bfloat16).reshape(experts, count, w_down.shape[1])
    returned = lax.all_to_all(answer, "ep", split_axis=0, concat_axis=0, tiled=True)
    weights = route_scale * gate_scores / jnp.sum(gate_scores, axis=1, keepdims=True)
    weighting = jnp.sum(
        jnp.where(places[None, None, :] == target[:, :, None], weights[:, :, None], 0.0), axis=1
    )
    answers = returned.reshape(experts * capacity, half_width).astype(jnp.float32)
    combined = jnp.dot(weighting, answers, precision=lax.Precision.HIGHEST)
    return combined.astype(jnp.bfloat16)


def prepare_kernel(experts, tokens, scores, ids, rows, perm):
    source = lax.broadcasted_iota(jnp.int32, (CHUNK, CHUNK), 0)
    place = lax.broadcasted_iota(jnp.int32, (CHUNK, CHUNK), 1)
    perm[...] = jnp.where((source & 3) * GROUP + (source >> 2) == place, 1.0, 0.0).astype(BF16)
    width = tokens.shape[1]
    for at in range(0, width, CHUNK):
        rows[:, at : at + CHUNK] = jnp.dot(
            tokens[:, at : at + CHUNK], perm[...], preferred_element_type=F32
        ).astype(BF16)
    weights = route_scale * scores[...] / jnp.sum(scores[...], axis=1, keepdims=True)
    lane = lax.broadcasted_iota(jnp.int32, (tokens.shape[0], EXTRA), 1)
    spread = jnp.zeros((tokens.shape[0], EXTRA), F32)
    for k in range(ids.shape[1]):
        spread += jnp.where(lane % experts == ids[:, k : k + 1], weights[:, k : k + 1], 0.0)
    high = spread.astype(BF16).astype(F32)
    mid = (spread - high).astype(BF16).astype(F32)
    low = spread - high - mid
    part = lane // experts
    rows[:, width:] = jnp.where(
        part == 0, high, jnp.where(part == 1, mid, jnp.where(part == 2, low, 0.0))
    ).astype(BF16)


def prepare(tokens, scores, ids, experts):
    n, width = tokens.shape
    return pl.pallas_call(
        functools.partial(prepare_kernel, experts),
        out_shape=(
            jax.ShapeDtypeStruct((n, width + EXTRA), BF16),
            jax.ShapeDtypeStruct((CHUNK, CHUNK), BF16),
        ),
        name="prepare",
    )(tokens, scores, ids)


def unpack_chunk(words, scale, zero, at, out, tiles, tile):
    sub = GROUP // WORD
    for t in range(tiles):
        cols = slice(t * tile, (t + 1) * tile)
        for g in range(WORD):
            s = scale[pl.ds(at * WORD + g, 1), cols]
            z = zero[pl.ds(at * WORD + g, 1), cols]
            w = words[g * sub : (g + 1) * sub, cols].astype(jnp.int32)
            for j in range(WORD):
                code = ((w >> (4 * j)) & 15).astype(F32)
                out[t, j * GROUP + g * sub : j * GROUP + (g + 1) * sub, :] = (
                    (code - z) * s
                ).astype(BF16)


def unpack_kernel(pairs, tiles, tile, *refs):
    ins, outs, scratch = refs[: 3 * pairs], refs[3 * pairs : 4 * pairs], refs[4 * pairs :]
    at = pl.program_id(0)

    @pl.when(at == 0)
    def _():
        for p in range(pairs):
            scratch[2 * p][...] = ins[3 * p + 1][...].astype(F32)
            scratch[2 * p + 1][...] = ins[3 * p + 2][...].astype(F32)

    for p in range(pairs):
        unpack_chunk(
            ins[3 * p], scratch[2 * p], scratch[2 * p + 1], at, outs[p], tiles, tile
        )


def unpack(triples, tile):
    words, scale, _ = triples[0]
    n, cols = words.shape
    tiles = cols // tile
    steps = n // GROUP
    in_specs, args, scratch = [], [], []
    for w, s, z in triples:
        in_specs += [
            pl.BlockSpec((GROUP, cols), lambda i: (i, 0)),
            pl.BlockSpec(s.shape, lambda i: (0, 0)),
            pl.BlockSpec(z.shape, lambda i: (0, 0)),
        ]
        args += [w, s, z]
        scratch += [pltpu.VMEM(s.shape, F32), pltpu.VMEM(z.shape, F32)]
    return pl.pallas_call(
        functools.partial(unpack_kernel, len(triples), tiles, tile),
        grid=(steps,),
        in_specs=in_specs,
        out_specs=[pl.BlockSpec((tiles, CHUNK, tile), lambda i: (0, i, 0)) for _ in triples],
        out_shape=[jax.ShapeDtypeStruct((tiles, n * WORD, tile), BF16) for _ in triples],
        scratch_shapes=scratch,
        compiler_params=pltpu.CompilerParams(vmem_limit_bytes=40 * 1024 * 1024),
        cost_estimate=pl.CostEstimate(
            flops=n * cols * 24 * len(triples),
            bytes_accessed=n * cols * 12 * len(triples),
            transcendentals=0,
        ),
        name="unpack",
    )(*args)


def expert_kernel(
    experts, first, mine, x0, x1, x2, x3, perm, wg, wu, wd, keep, send, xs, hs, hp, col
):
    i = pl.program_id(0)
    n, width = x0.shape[0], x0.shape[1] - EXTRA
    half = first // 2

    @pl.when(i == 0)
    def _():
        for at, x in enumerate((x0, x1, x2, x3)):
            xs[at * n : (at + 1) * n, :] = x[:, :width]
            parts = x[:, width:].astype(F32)
            lane = lax.broadcasted_iota(jnp.int32, parts.shape, 1)
            parts = jnp.where(lane % experts == mine[0], parts, 0.0)
            col[at * n : (at + 1) * n, :] = jnp.sum(parts, axis=1, keepdims=True)

    @pl.when(i < first)
    def _():
        gate = jnp.dot(xs[...], wg[0], preferred_element_type=F32)
        up = jnp.dot(xs[...], wu[0], preferred_element_type=F32)
        hs[i] = (gate / (1.0 + jnp.exp(-gate)) * up).astype(BF16)

    @pl.when(i == first)
    def _():
        tile = hs.shape[2]
        each = CHUNK // tile
        for c in range(first // each):
            total = None
            for b in range(each):
                part = jnp.dot(
                    hs[c * each + b], perm[b * tile : (b + 1) * tile, :], preferred_element_type=F32
                )
                total = part if total is None else total + part
            hp[:, c * CHUNK : (c + 1) * CHUNK] = total.astype(BF16)

    @pl.when(i >= first)
    def _():
        answer = jnp.dot(hp[...], wd[0], preferred_element_type=F32) * col[...]
        keep[...] = answer[: 2 * n].astype(BF16)
        send[...] = answer[2 * n :].astype(BF16)


def expert_block(mine, shards, perm, wg, wu, wd, experts):
    n, wide = shards[0].shape
    width = wide - EXTRA
    first, _, tile = wg.shape
    second, hidden, otile = wd.shape
    whole = lambda a: pl.BlockSpec(a.shape, lambda i: (0,) * a.ndim)
    flops = 2 * 4 * n * width * hidden * 3
    return pl.pallas_call(
        functools.partial(expert_kernel, experts, first),
        grid=(first + second,),
        in_specs=[pl.BlockSpec(memory_space=pltpu.SMEM)]
        + [whole(s) for s in shards]
        + [
            whole(perm),
            pl.BlockSpec((1, width, tile), lambda i: (jnp.minimum(i, first - 1), 0, 0)),
            pl.BlockSpec((1, width, tile), lambda i: (jnp.minimum(i, first - 1), 0, 0)),
            pl.BlockSpec((1, hidden, otile), lambda i: (jnp.maximum(i - first, 0), 0, 0)),
        ],
        out_specs=[
            pl.BlockSpec((2 * n, otile), lambda i: (0, jnp.maximum(i - first, 0))),
            pl.BlockSpec((2 * n, otile), lambda i: (0, jnp.maximum(i - first, 0))),
        ],
        out_shape=[jax.ShapeDtypeStruct((2 * n, width), BF16)] * 2,
        scratch_shapes=[
            pltpu.VMEM((4 * n, width), BF16),
            pltpu.VMEM((first, 4 * n, tile), BF16),
            pltpu.VMEM((4 * n, hidden), BF16),
            pltpu.VMEM((4 * n, 1), F32),
        ],
        compiler_params=pltpu.CompilerParams(vmem_limit_bytes=40 * 1024 * 1024),
        cost_estimate=pl.CostEstimate(
            flops=flops,
            bytes_accessed=3 * width * hidden * 2,
            transcendentals=4 * n * hidden,
        ),
        name="expert_block",
    )(mine, *shards, perm, wg, wu, wd)


def dense(
    tokens,
    gate_scores,
    route_ids,
    gate_codes,
    up_codes,
    down_codes,
    gate_scale,
    up_scale,
    down_scale,
    gate_zero,
    up_zero,
    down_zero,
):
    experts = lax.axis_size("ep")
    planes = experts // 4
    n = tokens.shape[0]
    mine = lax.axis_index("ep").astype(jnp.int32).reshape(1)

    def swap(value, bits):
        return lax.ppermute(value, "ep", [(i, i ^ bits) for i in range(experts)])

    rows, perm = prepare(tokens, gate_scores, route_ids, experts)
    w_gate, w_up = unpack(
        [(gate_codes[0], gate_scale[0], gate_zero[0]), (up_codes[0], up_scale[0], up_zero[0])], 256
    )
    (w_down,) = unpack([(down_codes[0], down_scale[0], down_zero[0])], 512)

    total = None
    for k in range(planes):
        here = rows if k == 0 else swap(rows, 4 * k)
        across = swap(here, 2)
        shards = [here, across, swap(here, 1), swap(across, 1)]
        keep, send = expert_block(mine, shards, perm, w_gate, w_up, w_down, experts)
        pair = keep.astype(F32) + swap(send, 1).astype(F32)
        plane = pair[:n] + swap(pair[n:].astype(BF16), 2).astype(F32)
        back = plane if k == 0 else swap(plane.astype(BF16), 4 * k).astype(F32)
        total = back if total is None else total + back
    return total.astype(BF16)


def solution(mesh):
    in_specs = (
        P(("grp", "ep"), "tp"),
        P(("grp", "ep"), None),
        P(("grp", "ep"), None),
        P("ep", None, "tp"),
        P("ep", None, "tp"),
        P("ep", None, "tp"),
        P("ep", None, "tp"),
        P("ep", None, "tp"),
        P("ep", None, "tp"),
        P("ep", None, "tp"),
        P("ep", None, "tp"),
        P("ep", None, "tp"),
    )
    out_specs = P(("grp", "ep"), "tp")
    experts = mesh.shape["ep"]
    few = mesh.shape["tp"] == 1 and experts % 4 == 0 and 3 * experts <= EXTRA
    return jax.shard_map(
        dense if few and experts & (experts - 1) == 0 else routed,
        mesh=mesh,
        in_specs=in_specs,
        out_specs=out_specs,
        check_vma=False,
    )
```

```python
import functools

import jax
import jax.numpy as jnp
from jax import lax
from jax.experimental import pallas as pl
from jax.experimental.pallas import tpu as pltpu
from jax.sharding import PartitionSpec as P

route_scale = 2.5
GROUP = 128
WORD = 4
CHUNK = GROUP * WORD
EXTRA = 128
QUARTERS = 4
F32 = jnp.float32
BF16 = jnp.bfloat16


def dequantize(words, scales, zeros):
    groups = scales.shape[0]
    packed = words.reshape(groups, words.shape[0] // groups, 1, words.shape[1])
    powers = jnp.array([1.0, 16.0, 256.0, 4096.0], jnp.float32)[None, None, :, None]
    lower = jnp.floor(packed / powers)
    higher = jnp.floor(packed / (16.0 * powers))
    codes = lower - 16.0 * higher
    values = (codes - zeros.astype(jnp.float32)[:, None, None, :]) * scales.astype(jnp.float32)[
        :, None, None, :
    ]
    return values.reshape(-1, words.shape[1]).astype(jnp.bfloat16)


def routed(
    tokens,
    gate_scores,
    route_ids,
    gate_codes,
    up_codes,
    down_codes,
    gate_scale,
    up_scale,
    down_scale,
    gate_zero,
    up_zero,
    down_zero,
):
    experts = lax.axis_size("ep")
    tok_rows, half_width = tokens.shape
    topk = route_ids.shape[1]
    capacity = min(tok_rows, max(2, 5 * tok_rows * topk // (4 * experts)))
    w_gate = dequantize(gate_codes[0], gate_scale[0], gate_zero[0])
    w_up = dequantize(up_codes[0], up_scale[0], up_zero[0])
    w_down = dequantize(down_codes[0], down_scale[0], down_zero[0])
    flat_ids = route_ids.reshape(-1)
    onehot = (flat_ids[:, None] == jnp.arange(experts, dtype=jnp.int32)[None, :]).astype(jnp.int32)
    earlier = jnp.cumsum(onehot, axis=0) - onehot
    slot = jnp.sum(earlier * onehot, axis=1)
    target = (flat_ids * capacity + slot).reshape(tok_rows, topk)
    places = jnp.arange(experts * capacity, dtype=jnp.int32)
    selector = jnp.sum(
        (places[:, None, None] == target[None, :, :]).astype(jnp.float32), axis=2
    ).astype(jnp.bfloat16)
    outgoing = jnp.dot(selector, tokens, preferred_element_type=jnp.float32).astype(jnp.bfloat16)
    outgoing = outgoing.reshape(experts, capacity, half_width)
    whole = lax.all_gather(
        lax.all_to_all(outgoing, "ep", split_axis=0, concat_axis=0, tiled=True),
        "tp",
        axis=2,
        tiled=True,
    )
    count = whole.shape[1]
    flat_rows = whole.reshape(-1, whole.shape[2])
    gate = jnp.dot(flat_rows, w_gate, preferred_element_type=jnp.float32)
    up = jnp.dot(flat_rows, w_up, preferred_element_type=jnp.float32)
    hidden = (jax.nn.silu(gate) * up).astype(jnp.bfloat16)
    summed = jnp.dot(
        lax.all_gather(hidden, "tp", axis=1, tiled=True), w_down, preferred_element_type=jnp.float32
    )
    answer = summed.astype(jnp.bfloat16).reshape(experts, count, w_down.shape[1])
    returned = lax.all_to_all(answer, "ep", split_axis=0, concat_axis=0, tiled=True)
    weights = route_scale * gate_scores / jnp.sum(gate_scores, axis=1, keepdims=True)
    weighting = jnp.sum(
        jnp.where(places[None, None, :] == target[:, :, None], weights[:, :, None], 0.0), axis=1
    )
    answers = returned.reshape(experts * capacity, half_width).astype(jnp.float32)
    combined = jnp.dot(weighting, answers, precision=lax.Precision.HIGHEST)
    return combined.astype(jnp.bfloat16)


def prepare_kernel(experts, tokens, scores, ids, rows, perm):
    source = lax.broadcasted_iota(jnp.int32, (CHUNK, CHUNK), 0)
    place = lax.broadcasted_iota(jnp.int32, (CHUNK, CHUNK), 1)
    perm[...] = jnp.where((source & 3) * GROUP + (source >> 2) == place, 1.0, 0.0).astype(BF16)
    width = tokens.shape[1]
    for at in range(0, width, CHUNK):
        rows[:, at : at + CHUNK] = jnp.dot(
            tokens[:, at : at + CHUNK], perm[...], preferred_element_type=F32
        ).astype(BF16)
    weights = route_scale * scores[...] / jnp.sum(scores[...], axis=1, keepdims=True)
    lane = lax.broadcasted_iota(jnp.int32, (tokens.shape[0], EXTRA), 1)
    spread = jnp.zeros((tokens.shape[0], EXTRA), F32)
    for k in range(ids.shape[1]):
        spread += jnp.where(lane % experts == ids[:, k : k + 1], weights[:, k : k + 1], 0.0)
    high = spread.astype(BF16).astype(F32)
    mid = (spread - high).astype(BF16).astype(F32)
    low = spread - high - mid
    part = lane // experts
    rows[:, width:] = jnp.where(
        part == 0, high, jnp.where(part == 1, mid, jnp.where(part == 2, low, 0.0))
    ).astype(BF16)


def prepare(tokens, scores, ids, experts):
    n, width = tokens.shape
    return pl.pallas_call(
        functools.partial(prepare_kernel, experts),
        out_shape=(
            jax.ShapeDtypeStruct((n, width + EXTRA), BF16),
            jax.ShapeDtypeStruct((CHUNK, CHUNK), BF16),
        ),
        compiler_params=pltpu.CompilerParams(vmem_limit_bytes=8 * 1024 * 1024),
        name="prepare",
    )(tokens, scores, ids)


def unpack_chunk(words, scale, zero, at, out, tiles, tile):
    sub = GROUP // WORD
    for t in range(tiles):
        cols = slice(t * tile, (t + 1) * tile)
        for g in range(WORD):
            s = scale[pl.ds(at * WORD + g, 1), cols]
            z = zero[pl.ds(at * WORD + g, 1), cols]
            w = words[g * sub : (g + 1) * sub, cols].astype(jnp.int32)
            for j in range(WORD):
                code = ((w >> (4 * j)) & 15).astype(F32)
                out[t, pl.ds(pl.multiple_of(at * CHUNK + j * GROUP + g * sub, sub), sub), :] = (
                    (code - z) * s
                ).astype(BF16)


def unpack_kernel(pairs, tiles, tile, *refs):
    ins, outs, scratch = refs[: 3 * pairs], refs[3 * pairs : 4 * pairs], refs[4 * pairs + 1 :]
    refs[4 * pairs][...] = jnp.zeros(refs[4 * pairs].shape, F32)
    at = pl.program_id(0)

    @pl.when(at == 0)
    def _():
        for p in range(pairs):
            scratch[2 * p][...] = ins[3 * p + 1][...].astype(F32)
            scratch[2 * p + 1][...] = ins[3 * p + 2][...].astype(F32)

    for p in range(pairs):
        unpack_chunk(
            ins[3 * p], scratch[2 * p], scratch[2 * p + 1], at, outs[p], tiles, tile
        )


def unpack(triples, tile):
    words, scale, _ = triples[0]
    n, cols = words.shape
    tiles = cols // tile
    steps = n // GROUP
    in_specs, args, scratch = [], [], []
    for w, s, z in triples:
        in_specs += [
            pl.BlockSpec((GROUP, cols), lambda i: (i, 0)),
            pl.BlockSpec(s.shape, lambda i: (0, 0)),
            pl.BlockSpec(z.shape, lambda i: (0, 0)),
        ]
        args += [w, s, z]
        scratch += [pltpu.VMEM(s.shape, F32), pltpu.VMEM(z.shape, F32)]
    return pl.pallas_call(
        functools.partial(unpack_kernel, len(triples), tiles, tile),
        grid=(steps,),
        in_specs=in_specs,
        out_specs=[pl.BlockSpec(memory_space=pltpu.VMEM) for _ in triples]
        + [pl.BlockSpec((8, 128), lambda i: (0, 0))],
        out_shape=[pltpu.VMEM((tiles, n * WORD, tile), BF16) for _ in triples]
        + [jax.ShapeDtypeStruct((8, 128), F32)],
        scratch_shapes=scratch,
        compiler_params=pltpu.CompilerParams(vmem_limit_bytes=20 * 1024 * 1024),
        cost_estimate=pl.CostEstimate(
            flops=n * cols * 24 * len(triples),
            bytes_accessed=n * cols * 4 * len(triples),
            transcendentals=0,
        ),
        name="unpack",
    )(*args)


def expert_kernel(
    experts, quarter, first, mine, near, cross, other, z, x, c, perm, wg, wu, wd,
    keep_near, keep_far, send_near, send_far, done, xs, hs, hp, col,
):
    i = pl.program_id(0)
    width = near.shape[1] - EXTRA
    far = z.shape[0]
    u = far // 3

    @pl.when(i == 0)
    def _():
        done[...] = jnp.zeros(done.shape, F32)
        mine_at = quarter * u
        n = near.shape[0]
        at = 0
        for ref, begin, count in (
            (near, mine_at, u),
            (cross, mine_at, u),
            (z, 0, far),
            (x, 0, far),
            (other, mine_at, u),
            (other, n + mine_at, u),
            (c, 0, 2 * far),
        ):
            xs[at : at + count, :] = ref[begin : begin + count, :width]
            parts = ref[begin : begin + count, width:].astype(F32)
            lane = lax.broadcasted_iota(jnp.int32, parts.shape, 1)
            parts = jnp.where(lane % experts == mine[0], parts, 0.0)
            col[at : at + count, :] = jnp.sum(parts, axis=1, keepdims=True)
            at += count

    @pl.when(i < first)
    def _():
        gate = jnp.dot(xs[...], wg[i], preferred_element_type=F32)
        up = jnp.dot(xs[...], wu[i], preferred_element_type=F32)
        hs[i] = (gate / (1.0 + jnp.exp(-gate)) * up).astype(BF16)

    @pl.when(i == first)
    def _():
        tile = hs.shape[2]
        each = CHUNK // tile
        for c in range(first // each):
            total = None
            for b in range(each):
                part = jnp.dot(
                    hs[c * each + b], perm[b * tile : (b + 1) * tile, :], preferred_element_type=F32
                )
                total = part if total is None else total + part
            hp[:, c * CHUNK : (c + 1) * CHUNK] = total.astype(BF16)

    @pl.when(i >= first)
    def _():
        answer = (jnp.dot(hp[...], wd[i - first], preferred_element_type=F32) * col[...]).astype(BF16)
        at = 0
        for ref in (keep_near, keep_far, send_near, send_far):
            ref[...] = answer[at : at + ref.shape[0]]
            at += ref.shape[0]


def expert_block(quarter, mine, near, cross, other, z, x, c, perm, wg, wu, wd, experts):
    far, wide = z.shape
    u = far // 3
    width = wide - EXTRA
    first, _, tile = wg.shape
    second, hidden, otile = wd.shape
    rows = 16 * u
    resident = pl.BlockSpec(memory_space=pltpu.VMEM)
    out = lambda n: pl.BlockSpec((n, otile), lambda i: (0, jnp.maximum(i - first, 0)))
    return pl.pallas_call(
        functools.partial(expert_kernel, experts, quarter, first),
        grid=(first + second,),
        in_specs=[pl.BlockSpec(memory_space=pltpu.SMEM)] + [resident] * 10,
        out_specs=[out(2 * u), out(6 * u), out(2 * u), out(6 * u)]
        + [pl.BlockSpec((8, 128), lambda i: (0, 0))],
        out_shape=[jax.ShapeDtypeStruct((n * u, width), BF16) for n in (2, 6, 2, 6)]
        + [jax.ShapeDtypeStruct((8, 128), F32)],
        scratch_shapes=[
            pltpu.VMEM((rows, width), BF16),
            pltpu.VMEM((first, rows, tile), BF16),
            pltpu.VMEM((rows, hidden), BF16),
            pltpu.VMEM((rows, 1), F32),
        ],
        compiler_params=pltpu.CompilerParams(vmem_limit_bytes=16 * 1024 * 1024),
        cost_estimate=pl.CostEstimate(
            flops=2 * rows * width * hidden * 3,
            bytes_accessed=rows * width * 4,
            transcendentals=rows * hidden,
        ),
        name="expert_block",
    )(mine, near, cross, other, z, x, c, perm, wg, wu, wd)


def dense(
    tokens,
    gate_scores,
    route_ids,
    gate_codes,
    up_codes,
    down_codes,
    gate_scale,
    up_scale,
    down_scale,
    gate_zero,
    up_zero,
    down_zero,
):
    experts = lax.axis_size("ep")
    n = tokens.shape[0]
    u = n // QUARTERS
    mine = lax.axis_index("ep").astype(jnp.int32).reshape(1)

    def swap(value, bits):
        return lax.ppermute(value, "ep", [(i, i ^ bits) for i in range(experts)])

    def after(values, *others):
        return lax.optimization_barrier((values, others))[0]

    quarters = range(QUARTERS)
    rows, perm = prepare(tokens, gate_scores, route_ids, experts)
    w_gate, w_up, done_in = unpack(
        [(gate_codes[0], gate_scale[0], gate_zero[0]), (up_codes[0], up_scale[0], up_zero[0])], 256
    )
    w_down, done_out = unpack([(down_codes[0], down_scale[0], down_zero[0])], 512)

    mids = [rows[q * u : (q + 1) * u] for q in quarters]
    twos = [swap(mids[q], 8) for q in quarters]
    cross = swap(rows, 2)
    twos, cross = after((twos, cross), done_in, done_out)
    ones = [swap(jnp.concatenate([mids[q], twos[q]]), 4) for q in quarters]
    other = swap(jnp.concatenate([rows, cross]), 1)
    z = [jnp.concatenate([ones[q], twos[q]]) for q in quarters]
    x = [swap(z[q], 2) for q in quarters]

    near, pairs, crossed, planes, back_one = [], [], [], [], []
    sums = [None] * QUARTERS

    def after_core(q):
        keep, send = sent[q]
        pair = keep.astype(F32) + send.astype(F32)
        crossing = pair[3 * u :].astype(BF16)
        pairs.append(pair[: 3 * u])
        crossed.append(swap(crossing, 2))
        return crossing

    def after_x(q):
        plane = pairs[q] + crossed[q].astype(F32)
        leaving = plane[: 2 * u].astype(BF16)
        planes.append(plane[2 * u :])
        back_one.append(swap(leaving, 4))
        return leaving

    def after_one(q):
        got = back_one[q].astype(F32)
        leaving = (planes[q] + got[u:]).astype(BF16)
        sums[q] = got[:u] + swap(leaving, 8).astype(F32)
        return leaving

    sent, done = [], None
    for q in quarters:
        zq, xq = (z[q], x[q]) if done is None else after((z[q], x[q]), done)
        c = swap(jnp.concatenate([zq, xq]), 1)
        due = [x[q + 1]] if q + 1 < QUARTERS else []
        if q == 0:
            due += [z[i] for i in quarters]
        if q >= 2:
            due.append(after_core(q - 2))
        if q >= 3:
            due.append(after_x(q - 3))
        if due:
            c = after(c, *due)
        keep_near, keep_far, send_near, send_far, done = expert_block(
            q, mine, rows, cross, other, zq, xq, c, perm, w_gate, w_up, w_down, experts
        )
        near.append((keep_near, send_near))
        sent.append((keep_far, swap(send_far, 1)))
    for q in range(max(QUARTERS - 2, 0), QUARTERS):
        after_core(q)
    for q in range(max(QUARTERS - 3, 0), QUARTERS):
        after_x(q)
    for q in quarters:
        after_one(q)
    sends = [s for _, s in near]
    got = swap(jnp.concatenate([s[:u] for s in sends] + [s[u:] for s in sends]), 1)
    kept = [k for k, _ in near]
    pair = jnp.concatenate([k[:u] for k in kept] + [k[u:] for k in kept]).astype(F32) + got.astype(F32)
    total = pair[:n] + swap(pair[n:].astype(BF16), 2).astype(F32) + jnp.concatenate(sums)
    return total.astype(BF16)


def solution(mesh):
    in_specs = (
        P(("grp", "ep"), "tp"),
        P(("grp", "ep"), None),
        P(("grp", "ep"), None),
        P("ep", None, "tp"),
        P("ep", None, "tp"),
        P("ep", None, "tp"),
        P("ep", None, "tp"),
        P("ep", None, "tp"),
        P("ep", None, "tp"),
        P("ep", None, "tp"),
        P("ep", None, "tp"),
        P("ep", None, "tp"),
    )
    out_specs = P(("grp", "ep"), "tp")
    experts = mesh.shape["ep"]
    few = mesh.shape["tp"] == 1 and experts == 16
    return jax.shard_map(
        dense if few else routed,
        mesh=mesh,
        in_specs=in_specs,
        out_specs=out_specs,
        check_vma=False,
    )
```

```python
import functools

import jax
import jax.numpy as jnp
from jax import lax
from jax.experimental import pallas as pl
from jax.experimental.pallas import tpu as pltpu
from jax.sharding import PartitionSpec as P

route_scale = 2.5
GROUP = 128
WORD = 4
CHUNK = GROUP * WORD
EXTRA = 128
QUARTERS = 4
F32 = jnp.float32
BF16 = jnp.bfloat16


def dequantize(words, scales, zeros):
    groups = scales.shape[0]
    packed = words.reshape(groups, words.shape[0] // groups, 1, words.shape[1])
    powers = jnp.array([1.0, 16.0, 256.0, 4096.0], jnp.float32)[None, None, :, None]
    lower = jnp.floor(packed / powers)
    higher = jnp.floor(packed / (16.0 * powers))
    codes = lower - 16.0 * higher
    values = (codes - zeros.astype(jnp.float32)[:, None, None, :]) * scales.astype(jnp.float32)[
        :, None, None, :
    ]
    return values.reshape(-1, words.shape[1]).astype(jnp.bfloat16)


def routed(
    tokens,
    gate_scores,
    route_ids,
    gate_codes,
    up_codes,
    down_codes,
    gate_scale,
    up_scale,
    down_scale,
    gate_zero,
    up_zero,
    down_zero,
):
    experts = lax.axis_size("ep")
    tok_rows, half_width = tokens.shape
    topk = route_ids.shape[1]
    capacity = min(tok_rows, max(2, 5 * tok_rows * topk // (4 * experts)))
    w_gate = dequantize(gate_codes[0], gate_scale[0], gate_zero[0])
    w_up = dequantize(up_codes[0], up_scale[0], up_zero[0])
    w_down = dequantize(down_codes[0], down_scale[0], down_zero[0])
    flat_ids = route_ids.reshape(-1)
    onehot = (flat_ids[:, None] == jnp.arange(experts, dtype=jnp.int32)[None, :]).astype(jnp.int32)
    earlier = jnp.cumsum(onehot, axis=0) - onehot
    slot = jnp.sum(earlier * onehot, axis=1)
    target = (flat_ids * capacity + slot).reshape(tok_rows, topk)
    places = jnp.arange(experts * capacity, dtype=jnp.int32)
    selector = jnp.sum(
        (places[:, None, None] == target[None, :, :]).astype(jnp.float32), axis=2
    ).astype(jnp.bfloat16)
    outgoing = jnp.dot(selector, tokens, preferred_element_type=jnp.float32).astype(jnp.bfloat16)
    outgoing = outgoing.reshape(experts, capacity, half_width)
    whole = lax.all_gather(
        lax.all_to_all(outgoing, "ep", split_axis=0, concat_axis=0, tiled=True),
        "tp",
        axis=2,
        tiled=True,
    )
    count = whole.shape[1]
    flat_rows = whole.reshape(-1, whole.shape[2])
    gate = jnp.dot(flat_rows, w_gate, preferred_element_type=jnp.float32)
    up = jnp.dot(flat_rows, w_up, preferred_element_type=jnp.float32)
    hidden = (jax.nn.silu(gate) * up).astype(jnp.bfloat16)
    summed = jnp.dot(
        lax.all_gather(hidden, "tp", axis=1, tiled=True), w_down, preferred_element_type=jnp.float32
    )
    answer = summed.astype(jnp.bfloat16).reshape(experts, count, w_down.shape[1])
    returned = lax.all_to_all(answer, "ep", split_axis=0, concat_axis=0, tiled=True)
    weights = route_scale * gate_scores / jnp.sum(gate_scores, axis=1, keepdims=True)
    weighting = jnp.sum(
        jnp.where(places[None, None, :] == target[:, :, None], weights[:, :, None], 0.0), axis=1
    )
    answers = returned.reshape(experts * capacity, half_width).astype(jnp.float32)
    combined = jnp.dot(weighting, answers, precision=lax.Precision.HIGHEST)
    return combined.astype(jnp.bfloat16)


def prepare_kernel(experts, mine, tokens, scores, ids, rows, perm, index):
    index[0] = mine[0]
    source = lax.broadcasted_iota(jnp.int32, (CHUNK, CHUNK), 0)
    place = lax.broadcasted_iota(jnp.int32, (CHUNK, CHUNK), 1)
    perm[...] = jnp.where((source & 3) * GROUP + (source >> 2) == place, 1.0, 0.0).astype(BF16)
    width = tokens.shape[1]
    for at in range(0, width, CHUNK):
        rows[:, at : at + CHUNK] = jnp.dot(
            tokens[:, at : at + CHUNK], perm[...], preferred_element_type=F32
        ).astype(BF16)
    weights = route_scale * scores[...] / jnp.sum(scores[...], axis=1, keepdims=True)
    lane = lax.broadcasted_iota(jnp.int32, (tokens.shape[0], EXTRA), 1)
    spread = jnp.zeros((tokens.shape[0], EXTRA), F32)
    for k in range(ids.shape[1]):
        spread += jnp.where(lane % experts == ids[:, k : k + 1], weights[:, k : k + 1], 0.0)
    high = spread.astype(BF16).astype(F32)
    mid = (spread - high).astype(BF16).astype(F32)
    low = spread - high - mid
    part = lane // experts
    rows[:, width:] = jnp.where(
        part == 0, high, jnp.where(part == 1, mid, jnp.where(part == 2, low, 0.0))
    ).astype(BF16)


def prepare(mine, tokens, scores, ids, experts):
    n, width = tokens.shape
    smem, vmem = pl.BlockSpec(memory_space=pltpu.SMEM), pl.BlockSpec(memory_space=pltpu.VMEM)
    return pl.pallas_call(
        functools.partial(prepare_kernel, experts),
        out_shape=(
            jax.ShapeDtypeStruct((n, width + EXTRA), BF16),
            jax.ShapeDtypeStruct((CHUNK, CHUNK), BF16),
            jax.ShapeDtypeStruct((1,), jnp.int32),
        ),
        in_specs=[smem, vmem, vmem, vmem],
        out_specs=(vmem, vmem, smem),
        compiler_params=pltpu.CompilerParams(vmem_limit_bytes=12 * 1024 * 1024),
        name="prepare",
    )(mine, tokens, scores, ids)


def unpack_kernel(later, words, scale, zero, *refs):
    out, done, scales, zeros, held, arrived = refs[later:]
    at = pl.program_id(0)
    sub = GROUP // WORD
    tiles, _, tile = out.shape

    def fetch(i):
        rows = slice(i * GROUP, (i + 1) * GROUP)
        return pltpu.make_async_copy(words.at[rows], held.at[i], arrived.at[i])

    @pl.when(at == 0)
    def _():
        for i in range(held.shape[0]):
            fetch(i).start()
        scales[...] = scale[...].astype(F32)
        zeros[...] = zero[...].astype(F32)
        done[...] = jnp.zeros(done.shape, F32)

    for i in range(held.shape[0]):

        @pl.when(at == i)
        def _():
            fetch(i).wait()

    for t in range(tiles):
        cols = slice(t * tile, (t + 1) * tile)
        for g in range(WORD):
            s = scales[pl.ds(at * WORD + g, 1), cols]
            z = zeros[pl.ds(at * WORD + g, 1), cols]
            w = held[at, g * sub : (g + 1) * sub, cols].astype(jnp.int32)
            for j in range(WORD):
                code = ((w >> (4 * j)) & 15).astype(F32)
                begin = pl.multiple_of(at * CHUNK + j * GROUP + g * sub, sub)
                out[t, pl.ds(begin, sub), :] = ((code - z) * s).astype(BF16)


def unpack(words, scale, zero, tile, before=()):
    n, cols = words.shape
    tiles, steps = cols // tile, n // GROUP
    words = pltpu.with_memory_space_constraint(words, pltpu.HBM)
    resident = pl.BlockSpec(memory_space=pltpu.VMEM)
    return pl.pallas_call(
        functools.partial(unpack_kernel, len(before)),
        grid=(steps,),
        in_specs=[pl.BlockSpec(memory_space=pl.ANY)] + [resident] * (2 + len(before)),
        out_specs=[resident] * 2,
        out_shape=[
            pltpu.VMEM((tiles, n * WORD, tile), BF16),
            jax.ShapeDtypeStruct((8, 128), F32),
        ],
        scratch_shapes=[
            pltpu.VMEM(scale.shape, F32),
            pltpu.VMEM(zero.shape, F32),
            pltpu.VMEM((steps, GROUP, cols), F32),
            pltpu.SemaphoreType.DMA((steps,)),
        ],
        compiler_params=pltpu.CompilerParams(vmem_limit_bytes=14 * 1024 * 1024),
        cost_estimate=pl.CostEstimate(
            flops=n * cols * 24, bytes_accessed=n * cols * 4, transcendentals=0
        ),
        name="unpack",
    )(words, scale, zero, *before)


def pack_kernel(cuts, *refs):
    out = refs[-1]
    at = 0
    for ref, (begin, count) in zip(refs, cuts):
        out[at : at + count, :] = ref[begin : begin + count, :]
        at += count


def pack(pieces, before=()):
    resident = pl.BlockSpec(memory_space=pltpu.VMEM)
    cuts = [(begin, count) for _, begin, count in pieces]
    rows = sum(count for _, count in cuts)
    return pl.pallas_call(
        functools.partial(pack_kernel, cuts),
        in_specs=[resident] * (len(pieces) + len(before)),
        out_specs=resident,
        out_shape=jax.ShapeDtypeStruct((rows, pieces[0][0].shape[1]), BF16),
        compiler_params=pltpu.CompilerParams(vmem_limit_bytes=4 * 1024 * 1024),
        cost_estimate=pl.CostEstimate(flops=0, bytes_accessed=rows * 4096, transcendentals=0),
        name="pack",
    )(*[p for p, _, _ in pieces], *before)


def join_kernel(later, keep, got, *refs):
    own, crossing = refs[later:]
    half = own.shape[0]
    own[...] = keep[:half].astype(F32) + got[:half].astype(F32)
    crossing[...] = (keep[half:].astype(F32) + got[half:].astype(F32)).astype(BF16)


def join(keep, got, before=()):
    resident = pl.BlockSpec(memory_space=pltpu.VMEM)
    rows, width = keep.shape
    return pl.pallas_call(
        functools.partial(join_kernel, len(before)),
        in_specs=[resident] * (2 + len(before)),
        out_specs=[resident] * 2,
        out_shape=[
            jax.ShapeDtypeStruct((rows // 2, width), F32),
            jax.ShapeDtypeStruct((rows // 2, width), BF16),
        ],
        compiler_params=pltpu.CompilerParams(vmem_limit_bytes=4 * 1024 * 1024),
        cost_estimate=pl.CostEstimate(flops=0, bytes_accessed=rows * 4096, transcendentals=0),
        name="join",
    )(keep, got, *before)


def land_kernel(parts, *refs):
    leaving, staying = refs[-2:]
    u = staying.shape[0] // parts
    for p in range(parts):
        own, got = refs[2 * p], refs[2 * p + 1]
        rows = lambda k: own[k * u : (k + 1) * u].astype(F32) + got[k * u : (k + 1) * u].astype(F32)
        leaving[2 * p * u : (2 * p + 1) * u, :] = rows(0).astype(BF16)
        leaving[(2 * p + 1) * u : (2 * p + 2) * u, :] = rows(2).astype(BF16)
        staying[p * u : (p + 1) * u, :] = rows(1)


def land(owns, gots, before=()):
    resident = pl.BlockSpec(memory_space=pltpu.VMEM)
    rows, width = owns[0].shape
    parts = len(owns)
    u = rows // 3
    pairs = [a for pair in zip(owns, gots) for a in pair]
    return pl.pallas_call(
        functools.partial(land_kernel, parts),
        in_specs=[resident] * (len(pairs) + len(before)),
        out_specs=[resident] * 2,
        out_shape=[
            jax.ShapeDtypeStruct((2 * parts * u, width), BF16),
            jax.ShapeDtypeStruct((parts * u, width), F32),
        ],
        compiler_params=pltpu.CompilerParams(vmem_limit_bytes=4 * 1024 * 1024),
        cost_estimate=pl.CostEstimate(flops=0, bytes_accessed=rows * 4096, transcendentals=0),
        name="land",
    )(*pairs, *before)


def expert_kernel(
    experts, quarter, first, later, mine, near, cross, other, z, x, c, perm, wg, wu, wd, *refs
):
    keep_near, keep_far, send_near, send_far, done, xs, hs, hp, col = refs[later:]
    i = pl.program_id(0)
    width = near.shape[1] - EXTRA
    far = z.shape[0]
    u = far // 3

    @pl.when(i == 0)
    def _():
        done[...] = jnp.zeros(done.shape, F32)
        mine_at = quarter * u
        n = near.shape[0]
        at = 0
        for ref, begin, count in (
            (near, mine_at, u),
            (cross, mine_at, u),
            (z, 0, far),
            (x, 0, far),
            (other, mine_at, u),
            (other, n + mine_at, u),
            (c, 0, 2 * far),
        ):
            xs[at : at + count, :] = ref[begin : begin + count, :width]
            parts = ref[begin : begin + count, width:].astype(F32)
            lane = lax.broadcasted_iota(jnp.int32, parts.shape, 1)
            parts = jnp.where(lane % experts == mine[0], parts, 0.0)
            col[at : at + count, :] = jnp.sum(parts, axis=1, keepdims=True)
            at += count

    @pl.when(i < first)
    def _():
        gate = jnp.dot(xs[...], wg[i], preferred_element_type=F32)
        up = jnp.dot(xs[...], wu[i], preferred_element_type=F32)
        hs[i] = (gate / (1.0 + jnp.exp(-gate)) * up).astype(BF16)

    @pl.when(i == first)
    def _():
        tile = hs.shape[2]
        each = CHUNK // tile
        for c in range(first // each):
            total = None
            for b in range(each):
                part = jnp.dot(
                    hs[c * each + b], perm[b * tile : (b + 1) * tile, :], preferred_element_type=F32
                )
                total = part if total is None else total + part
            hp[:, c * CHUNK : (c + 1) * CHUNK] = total.astype(BF16)

    @pl.when(i >= first)
    def _():
        answer = (jnp.dot(hp[...], wd[i - first], preferred_element_type=F32) * col[...]).astype(BF16)
        at = 0
        for ref in (keep_near, keep_far, send_near, send_far):
            ref[...] = answer[at : at + ref.shape[0]]
            at += ref.shape[0]


def expert_block(quarter, mine, near, cross, other, z, x, c, perm, wg, wu, wd, experts, before):
    far, wide = z.shape
    u = far // 3
    width = wide - EXTRA
    first, _, tile = wg.shape
    second, hidden, otile = wd.shape
    rows = 16 * u
    resident = pl.BlockSpec(memory_space=pltpu.VMEM)
    out = lambda n: pl.BlockSpec((n, otile), lambda i: (0, jnp.maximum(i - first, 0)))
    return pl.pallas_call(
        functools.partial(expert_kernel, experts, quarter, first, len(before)),
        grid=(first + second,),
        in_specs=[pl.BlockSpec(memory_space=pltpu.SMEM)] + [resident] * (10 + len(before)),
        out_specs=[out(2 * u), out(6 * u), out(2 * u), out(6 * u)]
        + [pl.BlockSpec(memory_space=pltpu.VMEM)],
        out_shape=[jax.ShapeDtypeStruct((n * u, width), BF16) for n in (2, 6, 2, 6)]
        + [jax.ShapeDtypeStruct((8, 128), F32)],
        scratch_shapes=[
            pltpu.VMEM((rows, width), BF16),
            pltpu.VMEM((first, rows, tile), BF16),
            pltpu.VMEM((rows, hidden), BF16),
            pltpu.VMEM((rows, 1), F32),
        ],
        compiler_params=pltpu.CompilerParams(vmem_limit_bytes=12 * 1024 * 1024),
        cost_estimate=pl.CostEstimate(
            flops=2 * rows * width * hidden * 3,
            bytes_accessed=rows * width * 4,
            transcendentals=rows * hidden,
        ),
        name="expert_block",
    )(mine, near, cross, other, z, x, c, perm, wg, wu, wd, *before)


def dense(
    tokens,
    gate_scores,
    route_ids,
    gate_codes,
    up_codes,
    down_codes,
    gate_scale,
    up_scale,
    down_scale,
    gate_zero,
    up_zero,
    down_zero,
):
    experts = lax.axis_size("ep")
    n = tokens.shape[0]
    u = n // QUARTERS
    mine = lax.axis_index("ep").astype(jnp.int32).reshape(1)

    def swap(value, bits):
        return lax.ppermute(value, "ep", [(i, i ^ bits) for i in range(experts)])

    quarters = range(QUARTERS)
    rows, perm, mine = prepare(mine, tokens, gate_scores, route_ids, experts)

    half = n // 2
    cross = swap(rows, 2)
    first = [swap(rows[:half], 4 * k) for k in range(1, 4)]
    two = swap(rows[half:], 8)
    w_down, done_down = unpack(down_codes[0], down_scale[0], down_zero[0], 1792)
    w_gate, done_gate = unpack(gate_codes[0], gate_scale[0], gate_zero[0], 512)
    w_up, done_up = unpack(up_codes[0], up_scale[0], up_zero[0], 512)
    unpacked = [done_down, done_gate, done_up]

    z = [pack([(first[k], q * u, u) for k in range(3)], unpacked + [two]) for q in range(2)]
    onward = pack([(rows, half, half), (two, 0, half)], unpacked)
    one = swap(onward, 4)
    other = swap(pack([(rows, 0, n), (cross, 0, n)], unpacked), 1)
    z += [pack([(one, q * u, u), (two, q * u, u), (one, half + q * u, u)]) for q in range(2)]
    x = [swap(v, 2) for v in z]
    both, done, near, back = [], [], [], []
    own, crossing, crossed = [None] * QUARTERS, [None] * QUARTERS, [None] * QUARTERS
    leaving, staying = [None] * QUARTERS, [None] * QUARTERS

    def start_core(q, before):
        both.append(pack([(z[q], 0, 3 * u), (x[q], 0, 3 * u)], before))

    def after_core(q, before):
        own[q], crossing[q] = join(near[q][1], back[q], before)
        crossed[q] = swap(crossing[q], 2)

    def after_x(q, before):
        leaving[q], staying[q] = land([own[q]], [crossed[q]], before)

    def expert(q, before):
        keep_near, keep_far, send_near, send_far, token = expert_block(
            q, mine, rows, cross, other, z[q], x[q], swap(both[q], 1), perm,
            w_gate, w_up, w_down, experts, before,
        )
        done.append(token)
        near.append((keep_near, keep_far, send_near))
        back.append(swap(send_far, 1))

    start_core(0, [z[2], z[3]])
    expert(0, [])
    start_core(1, done[-1:])
    start_core(2, done[-1:])
    expert(1, [both[2]])
    start_core(3, done[-1:])
    after_core(0, done[-1:])
    expert(2, [both[3], crossing[0]])
    after_core(1, done[-1:])
    after_x(0, done[-1:])
    expert(3, [crossing[1], leaving[0]])
    after_core(2, done[-1:])
    after_core(3, [crossing[2]])
    after_x(1, [crossing[3]])
    after_x(2, [leaving[1]])

    sends = [s for _, _, s in near]
    kept = [k for k, _, _ in near]
    send = pack([(s, 0, u) for s in sends] + [(s, u, u) for s in sends], done[-1:])
    keep = pack([(k, 0, u) for k in kept] + [(k, u, u) for k in kept], done[-1:])
    home, away = join(keep, swap(send, 1), [leaving[2]])
    away = swap(away, 2)
    after_x(3, [])
    sums = []
    for q in range(QUARTERS):
        got = swap(leaving[q], 4).astype(F32)
        last = swap((staying[q] + got[u:]).astype(BF16), 8).astype(F32)
        sums.append(got[:u] + last)
    total = home + away.astype(F32) + jnp.concatenate(sums)
    return total.astype(BF16)


def solution(mesh):
    in_specs = (
        P(("grp", "ep"), "tp"),
        P(("grp", "ep"), None),
        P(("grp", "ep"), None),
        P("ep", None, "tp"),
        P("ep", None, "tp"),
        P("ep", None, "tp"),
        P("ep", None, "tp"),
        P("ep", None, "tp"),
        P("ep", None, "tp"),
        P("ep", None, "tp"),
        P("ep", None, "tp"),
        P("ep", None, "tp"),
    )
    out_specs = P(("grp", "ep"), "tp")
    experts = mesh.shape["ep"]
    few = mesh.shape["tp"] == 1 and experts == 16
    return jax.shard_map(
        dense if few else routed,
        mesh=mesh,
        in_specs=in_specs,
        out_specs=out_specs,
        check_vma=False,
    )
```

```python
import functools

import jax
import jax.numpy as jnp
from jax import lax
from jax.experimental import pallas as pl
from jax.experimental.pallas import tpu as pltpu
from jax.sharding import PartitionSpec as P

route_scale = 2.5
GROUP = 128
WORD = 4
CHUNK = GROUP * WORD
EXTRA = 128
QUARTERS = 4
F32 = jnp.float32
BF16 = jnp.bfloat16


def dequantize(words, scales, zeros):
    groups = scales.shape[0]
    packed = words.reshape(groups, words.shape[0] // groups, 1, words.shape[1])
    powers = jnp.array([1.0, 16.0, 256.0, 4096.0], jnp.float32)[None, None, :, None]
    lower = jnp.floor(packed / powers)
    higher = jnp.floor(packed / (16.0 * powers))
    codes = lower - 16.0 * higher
    values = (codes - zeros.astype(jnp.float32)[:, None, None, :]) * scales.astype(jnp.float32)[
        :, None, None, :
    ]
    return values.reshape(-1, words.shape[1]).astype(jnp.bfloat16)


def routed(
    tokens,
    gate_scores,
    route_ids,
    gate_codes,
    up_codes,
    down_codes,
    gate_scale,
    up_scale,
    down_scale,
    gate_zero,
    up_zero,
    down_zero,
):
    experts = lax.axis_size("ep")
    tok_rows, half_width = tokens.shape
    topk = route_ids.shape[1]
    capacity = min(tok_rows, max(2, 5 * tok_rows * topk // (4 * experts)))
    w_gate = dequantize(gate_codes[0], gate_scale[0], gate_zero[0])
    w_up = dequantize(up_codes[0], up_scale[0], up_zero[0])
    w_down = dequantize(down_codes[0], down_scale[0], down_zero[0])
    flat_ids = route_ids.reshape(-1)
    onehot = (flat_ids[:, None] == jnp.arange(experts, dtype=jnp.int32)[None, :]).astype(jnp.int32)
    earlier = jnp.cumsum(onehot, axis=0) - onehot
    slot = jnp.sum(earlier * onehot, axis=1)
    target = (flat_ids * capacity + slot).reshape(tok_rows, topk)
    places = jnp.arange(experts * capacity, dtype=jnp.int32)
    selector = jnp.sum(
        (places[:, None, None] == target[None, :, :]).astype(jnp.float32), axis=2
    ).astype(jnp.bfloat16)
    outgoing = jnp.dot(selector, tokens, preferred_element_type=jnp.float32).astype(jnp.bfloat16)
    outgoing = outgoing.reshape(experts, capacity, half_width)
    whole = lax.all_gather(
        lax.all_to_all(outgoing, "ep", split_axis=0, concat_axis=0, tiled=True),
        "tp",
        axis=2,
        tiled=True,
    )
    count = whole.shape[1]
    flat_rows = whole.reshape(-1, whole.shape[2])
    gate = jnp.dot(flat_rows, w_gate, preferred_element_type=jnp.float32)
    up = jnp.dot(flat_rows, w_up, preferred_element_type=jnp.float32)
    hidden = (jax.nn.silu(gate) * up).astype(jnp.bfloat16)
    summed = jnp.dot(
        lax.all_gather(hidden, "tp", axis=1, tiled=True), w_down, preferred_element_type=jnp.float32
    )
    answer = summed.astype(jnp.bfloat16).reshape(experts, count, w_down.shape[1])
    returned = lax.all_to_all(answer, "ep", split_axis=0, concat_axis=0, tiled=True)
    weights = route_scale * gate_scores / jnp.sum(gate_scores, axis=1, keepdims=True)
    weighting = jnp.sum(
        jnp.where(places[None, None, :] == target[:, :, None], weights[:, :, None], 0.0), axis=1
    )
    answers = returned.reshape(experts * capacity, half_width).astype(jnp.float32)
    combined = jnp.dot(weighting, answers, precision=lax.Precision.HIGHEST)
    return combined.astype(jnp.bfloat16)


def prepare_kernel(experts, mine, tokens, scores, ids, rows, perm, index):
    index[0] = mine[0]
    source = lax.broadcasted_iota(jnp.int32, (CHUNK, CHUNK), 0)
    place = lax.broadcasted_iota(jnp.int32, (CHUNK, CHUNK), 1)
    perm[...] = jnp.where((source & 3) * GROUP + (source >> 2) == place, 1.0, 0.0).astype(BF16)
    width = tokens.shape[1]
    for at in range(0, width, CHUNK):
        rows[:, at : at + CHUNK] = jnp.dot(
            tokens[:, at : at + CHUNK], perm[...], preferred_element_type=F32
        ).astype(BF16)
    weights = route_scale * scores[...] / jnp.sum(scores[...], axis=1, keepdims=True)
    lane = lax.broadcasted_iota(jnp.int32, (tokens.shape[0], EXTRA), 1)
    spread = jnp.zeros((tokens.shape[0], EXTRA), F32)
    for k in range(ids.shape[1]):
        spread += jnp.where(lane % experts == ids[:, k : k + 1], weights[:, k : k + 1], 0.0)
    high = spread.astype(BF16).astype(F32)
    mid = (spread - high).astype(BF16).astype(F32)
    low = spread - high - mid
    part = lane // experts
    rows[:, width:] = jnp.where(
        part == 0, high, jnp.where(part == 1, mid, jnp.where(part == 2, low, 0.0))
    ).astype(BF16)


def prepare(mine, tokens, scores, ids, experts):
    n, width = tokens.shape
    smem, vmem = pl.BlockSpec(memory_space=pltpu.SMEM), pl.BlockSpec(memory_space=pltpu.VMEM)
    return pl.pallas_call(
        functools.partial(prepare_kernel, experts),
        out_shape=(
            jax.ShapeDtypeStruct((n, width + EXTRA), BF16),
            jax.ShapeDtypeStruct((CHUNK, CHUNK), BF16),
            jax.ShapeDtypeStruct((1,), jnp.int32),
        ),
        in_specs=[smem, vmem, vmem, vmem],
        out_specs=(vmem, vmem, smem),
        compiler_params=pltpu.CompilerParams(vmem_limit_bytes=12 * 1024 * 1024),
        name="prepare",
    )(mine, tokens, scores, ids)


def unpack_kernel(later, words, scale, zero, *refs):
    out, done, scales, zeros, held, arrived = refs[later:]
    at = pl.program_id(0)
    sub = GROUP // WORD
    tiles, _, tile = out.shape

    def fetch(i):
        rows = slice(i * GROUP, (i + 1) * GROUP)
        return pltpu.make_async_copy(words.at[rows], held.at[i], arrived.at[i])

    @pl.when(at == 0)
    def _():
        for i in range(held.shape[0]):
            fetch(i).start()
        scales[...] = scale[...].astype(F32)
        zeros[...] = zero[...].astype(F32)
        done[...] = jnp.zeros(done.shape, F32)

    for i in range(held.shape[0]):

        @pl.when(at == i)
        def _():
            fetch(i).wait()

    for t in range(tiles):
        cols = slice(t * tile, (t + 1) * tile)
        for g in range(WORD):
            s = scales[pl.ds(at * WORD + g, 1), cols]
            z = zeros[pl.ds(at * WORD + g, 1), cols]
            w = held[at, g * sub : (g + 1) * sub, cols].astype(jnp.int32)
            for j in range(WORD):
                code = ((w >> (4 * j)) & 15).astype(F32)
                begin = pl.multiple_of(at * CHUNK + j * GROUP + g * sub, sub)
                out[t, pl.ds(begin, sub), :] = ((code - z) * s).astype(BF16)


def unpack(words, scale, zero, tile, before=()):
    n, cols = words.shape
    tiles, steps = cols // tile, n // GROUP
    words = pltpu.with_memory_space_constraint(words, pltpu.HBM)
    resident = pl.BlockSpec(memory_space=pltpu.VMEM)
    return pl.pallas_call(
        functools.partial(unpack_kernel, len(before)),
        grid=(steps,),
        in_specs=[pl.BlockSpec(memory_space=pl.ANY)] + [resident] * (2 + len(before)),
        out_specs=[resident] * 2,
        out_shape=[
            pltpu.VMEM((tiles, n * WORD, tile), BF16),
            jax.ShapeDtypeStruct((8, 128), F32),
        ],
        scratch_shapes=[
            pltpu.VMEM(scale.shape, F32),
            pltpu.VMEM(zero.shape, F32),
            pltpu.VMEM((steps, GROUP, cols), F32),
            pltpu.SemaphoreType.DMA((steps,)),
        ],
        compiler_params=pltpu.CompilerParams(vmem_limit_bytes=14 * 1024 * 1024),
        cost_estimate=pl.CostEstimate(
            flops=n * cols * 24, bytes_accessed=n * cols * 4, transcendentals=0
        ),
        name="unpack",
    )(words, scale, zero, *before)


def pack_kernel(cuts, *refs):
    out = refs[-1]
    at = 0
    for ref, (begin, count) in zip(refs, cuts):
        out[at : at + count, :] = ref[begin : begin + count, :]
        at += count


def pack(pieces, before=()):
    resident = pl.BlockSpec(memory_space=pltpu.VMEM)
    cuts = [(begin, count) for _, begin, count in pieces]
    rows = sum(count for _, count in cuts)
    return pl.pallas_call(
        functools.partial(pack_kernel, cuts),
        in_specs=[resident] * (len(pieces) + len(before)),
        out_specs=resident,
        out_shape=jax.ShapeDtypeStruct((rows, pieces[0][0].shape[1]), BF16),
        compiler_params=pltpu.CompilerParams(vmem_limit_bytes=4 * 1024 * 1024),
        cost_estimate=pl.CostEstimate(flops=0, bytes_accessed=rows * 4096, transcendentals=0),
        name="pack",
    )(*[p for p, _, _ in pieces], *before)


def join_kernel(parts, *refs):
    own, crossing = refs[-2:]
    half = own.shape[0] // parts
    for p in range(parts):
        keep, got = refs[2 * p], refs[2 * p + 1]
        rows = slice(p * half, (p + 1) * half)
        own[rows, :] = keep[:half].astype(F32) + got[:half].astype(F32)
        crossing[rows, :] = (keep[half:].astype(F32) + got[half:].astype(F32)).astype(BF16)


def join(keeps, gots, before=()):
    resident = pl.BlockSpec(memory_space=pltpu.VMEM)
    rows, width = keeps[0].shape
    parts = len(keeps)
    pairs = [a for pair in zip(keeps, gots) for a in pair]
    return pl.pallas_call(
        functools.partial(join_kernel, parts),
        in_specs=[resident] * (len(pairs) + len(before)),
        out_specs=[resident] * 2,
        out_shape=[
            jax.ShapeDtypeStruct((parts * rows // 2, width), F32),
            jax.ShapeDtypeStruct((parts * rows // 2, width), BF16),
        ],
        compiler_params=pltpu.CompilerParams(vmem_limit_bytes=4 * 1024 * 1024),
        cost_estimate=pl.CostEstimate(flops=0, bytes_accessed=rows * 4096, transcendentals=0),
        name="join",
    )(*pairs, *before)


def land_kernel(parts, own, got, *refs):
    leaving, staying = refs[-2:]
    u = staying.shape[0] // parts
    for p in range(parts):
        sums = []
        for k in range(3):
            rows = slice((3 * p + k) * u, (3 * p + k + 1) * u)
            sums.append(own[rows].astype(F32) + got[rows].astype(F32))
        leaving[p * u : (p + 1) * u, :] = sums[0].astype(BF16)
        leaving[(parts + p) * u : (parts + p + 1) * u, :] = sums[2].astype(BF16)
        staying[p * u : (p + 1) * u, :] = sums[1]


def land(own, got, parts, before=()):
    resident = pl.BlockSpec(memory_space=pltpu.VMEM)
    rows, width = own.shape
    return pl.pallas_call(
        functools.partial(land_kernel, parts),
        in_specs=[resident] * (2 + len(before)),
        out_specs=[resident] * 2,
        out_shape=[
            jax.ShapeDtypeStruct((2 * rows // 3, width), BF16),
            jax.ShapeDtypeStruct((rows // 3, width), F32),
        ],
        compiler_params=pltpu.CompilerParams(vmem_limit_bytes=4 * 1024 * 1024),
        cost_estimate=pl.CostEstimate(flops=0, bytes_accessed=rows * 4096, transcendentals=0),
        name="land",
    )(own, got, *before)


def pass_kernel(staying, got, *refs):
    u = staying.shape[0]
    refs[-1][...] = (staying[...] + got[u:].astype(F32)).astype(BF16)


def pass_on(staying, got, before=()):
    resident = pl.BlockSpec(memory_space=pltpu.VMEM)
    return pl.pallas_call(
        pass_kernel,
        in_specs=[resident] * (2 + len(before)),
        out_specs=resident,
        out_shape=jax.ShapeDtypeStruct(staying.shape, BF16),
        compiler_params=pltpu.CompilerParams(vmem_limit_bytes=4 * 1024 * 1024),
        cost_estimate=pl.CostEstimate(
            flops=0, bytes_accessed=staying.shape[0] * 4096, transcendentals=0
        ),
        name="pass_on",
    )(staying, got, *before)


def expert_kernel(
    experts, quarter, first, later, mine, near, cross, other, z, x, c, perm, wg, wu, wd, *refs
):
    keep_near, keep_far, send_near, send_far, done, xs, hs, hp, col = refs[later:]
    i = pl.program_id(0)
    width = near.shape[1] - EXTRA
    far = z.shape[0]
    u = far // 3

    @pl.when(i == 0)
    def _():
        done[...] = jnp.zeros(done.shape, F32)
        mine_at = quarter * u
        n = near.shape[0]
        at = 0
        for ref, begin, count in (
            (near, mine_at, u),
            (cross, mine_at, u),
            (z, 0, far),
            (x, 0, far),
            (other, mine_at, u),
            (other, n + mine_at, u),
            (c, 0, 2 * far),
        ):
            xs[at : at + count, :] = ref[begin : begin + count, :width]
            parts = ref[begin : begin + count, width:].astype(F32)
            lane = lax.broadcasted_iota(jnp.int32, parts.shape, 1)
            parts = jnp.where(lane % experts == mine[0], parts, 0.0)
            col[at : at + count, :] = jnp.sum(parts, axis=1, keepdims=True)
            at += count

    @pl.when(i < first)
    def _():
        gate = jnp.dot(xs[...], wg[i], preferred_element_type=F32)
        up = jnp.dot(xs[...], wu[i], preferred_element_type=F32)
        hs[i] = (gate / (1.0 + jnp.exp(-gate)) * up).astype(BF16)

    @pl.when(i == first)
    def _():
        tile = hs.shape[2]
        each = CHUNK // tile
        for c in range(first // each):
            total = None
            for b in range(each):
                part = jnp.dot(
                    hs[c * each + b], perm[b * tile : (b + 1) * tile, :], preferred_element_type=F32
                )
                total = part if total is None else total + part
            hp[:, c * CHUNK : (c + 1) * CHUNK] = total.astype(BF16)

    @pl.when(i >= first)
    def _():
        answer = (jnp.dot(hp[...], wd[i - first], preferred_element_type=F32) * col[...]).astype(BF16)
        at = 0
        for ref in (keep_near, keep_far, send_near, send_far):
            ref[...] = answer[at : at + ref.shape[0]]
            at += ref.shape[0]


def expert_block(quarter, mine, near, cross, other, z, x, c, perm, wg, wu, wd, experts, before):
    far, wide = z.shape
    u = far // 3
    width = wide - EXTRA
    first, _, tile = wg.shape
    second, hidden, otile = wd.shape
    rows = 16 * u
    resident = pl.BlockSpec(memory_space=pltpu.VMEM)
    out = lambda n: pl.BlockSpec((n, otile), lambda i: (0, jnp.maximum(i - first, 0)))
    return pl.pallas_call(
        functools.partial(expert_kernel, experts, quarter, first, len(before)),
        grid=(first + second,),
        in_specs=[pl.BlockSpec(memory_space=pltpu.SMEM)] + [resident] * (10 + len(before)),
        out_specs=[out(2 * u), out(6 * u), out(2 * u), out(6 * u)]
        + [pl.BlockSpec(memory_space=pltpu.VMEM)],
        out_shape=[jax.ShapeDtypeStruct((n * u, width), BF16) for n in (2, 6, 2, 6)]
        + [jax.ShapeDtypeStruct((8, 128), F32)],
        scratch_shapes=[
            pltpu.VMEM((rows, width), BF16),
            pltpu.VMEM((first, rows, tile), BF16),
            pltpu.VMEM((rows, hidden), BF16),
            pltpu.VMEM((rows, 1), F32),
        ],
        compiler_params=pltpu.CompilerParams(vmem_limit_bytes=12 * 1024 * 1024),
        cost_estimate=pl.CostEstimate(
            flops=2 * rows * width * hidden * 3,
            bytes_accessed=rows * width * 4,
            transcendentals=rows * hidden,
        ),
        name="expert_block",
    )(mine, near, cross, other, z, x, c, perm, wg, wu, wd, *before)


def dense(
    tokens,
    gate_scores,
    route_ids,
    gate_codes,
    up_codes,
    down_codes,
    gate_scale,
    up_scale,
    down_scale,
    gate_zero,
    up_zero,
    down_zero,
):
    experts = lax.axis_size("ep")
    n = tokens.shape[0]
    u = n // QUARTERS
    mine = lax.axis_index("ep").astype(jnp.int32).reshape(1)

    def swap(value, bits):
        return lax.ppermute(value, "ep", [(i, i ^ bits) for i in range(experts)])

    quarters = range(QUARTERS)
    rows, perm, mine = prepare(mine, tokens, gate_scores, route_ids, experts)

    half = n // 2
    cross = swap(rows, 2)
    first = [swap(rows[:half], 4 * k) for k in range(1, 4)]
    two = swap(rows[half:], 8)
    w_down, done_down = unpack(down_codes[0], down_scale[0], down_zero[0], 1792)
    w_gate, done_gate = unpack(gate_codes[0], gate_scale[0], gate_zero[0], 512)
    w_up, done_up = unpack(up_codes[0], up_scale[0], up_zero[0], 512)
    unpacked = [done_down, done_gate, done_up]

    z = [pack([(first[k], q * u, u) for k in range(3)], unpacked + [two]) for q in range(2)]
    onward = pack([(rows, half, half), (two, 0, half)], unpacked)
    one = swap(onward, 4)
    other = swap(pack([(rows, 0, n), (cross, 0, n)], unpacked), 1)
    z += [pack([(one, q * u, u), (two, q * u, u), (one, half + q * u, u)]) for q in range(2)]
    two_x = swap(pack([(cross, 3 * u, u)], unpacked), 8)
    x = [swap(v, 2) for v in z[:3]]
    done, near, far, sent = [], [], [], []

    def expert(q, ahead, before):
        both = pack([(z[q], 0, 3 * u), (x[q], 0, 3 * u)], done[-1:] + ahead)
        keep_near, keep_far, send_near, send_far, token = expert_block(
            q, mine, rows, cross, other, z[q], x[q], swap(both, 1), perm,
            w_gate, w_up, w_down, experts, before,
        )
        done.append(token)
        near.append((keep_near, send_near))
        far.append(keep_far)
        sent.append(send_far)

    def after_core(q, before):
        own, crossing = join([far[q]], [swap(sent[q], 1)], before)
        return own, crossing, swap(crossing, 2)

    expert(0, [z[2], z[3]], [])
    onward_x = pack([(cross, 3 * u, u), (two_x, 0, u)], done[-1:])
    one_x = swap(onward_x, 4)
    leaving_0, staying_0 = land(far[0], swap(sent[0], 1), 2, done[-1:])
    expert(1, [onward_x], [leaving_0])
    x.append(pack([(one_x, 0, u), (two_x, 0, u), (one_x, u, u)], done[-1:]))
    own_1, crossing_1, crossed_1 = after_core(1, done[-1:])
    expert(2, [x[3]], [crossing_1])
    got_0 = swap(leaving_0, 4)
    passed_0 = pass_on(staying_0, got_0, done[-1:])
    leaving_1, staying_1 = land(own_1, crossed_1, 1, done[-1:])
    own_2, crossing_2, crossed_2 = after_core(2, done[-1:])
    expert(3, [passed_0, leaving_1], [crossing_2])
    got_1 = swap(leaving_1, 4)
    passed_1 = pass_on(staying_1, got_1, done[-1:])
    leaving_2, staying_2 = land(own_2, crossed_2, 1, done[-1:])
    sent[3] = pack([(sent[3], 0, 6 * u)], [passed_1, leaving_2])
    own_3, crossing_3, crossed_3 = after_core(3, done[-1:])
    leaving_3, staying_3 = land(own_3, crossed_3, 1)

    sends = [s for _, s in near]
    kept = [k for k, _ in near]
    send = pack([(s, 0, u) for s in sends] + [(s, u, u) for s in sends], done[-1:])
    keep = pack([(k, 0, u) for k in kept] + [(k, u, u) for k in kept], done[-1:])
    last_0 = swap(passed_0, 8)
    sum_0 = got_0[: 2 * u].astype(F32) + last_0.astype(F32)
    pair = keep.astype(F32) + swap(send, 1).astype(F32)
    away = jnp.concatenate([pair[n : n + u] + sum_0[u:], pair[n + u :]]).astype(BF16)
    over = [swap(away[:half], 2), swap(away[half:], 2)]
    got_2, got_3 = swap(leaving_2, 4), swap(leaving_3, 4)
    passed_2 = pass_on(staying_2, got_2, [crossing_3])
    passed_3 = pass_on(staying_3, got_3, [over[0]])
    sums = [sum_0[:u]]
    for got, passed in ((got_1, passed_1), (got_2, passed_2), (got_3, passed_3)):
        sums.append(got[:u].astype(F32) + swap(passed, 8).astype(F32))
    total = pair[:n] + jnp.concatenate(over).astype(F32) + jnp.concatenate(sums)
    return total.astype(BF16)


def solution(mesh):
    in_specs = (
        P(("grp", "ep"), "tp"),
        P(("grp", "ep"), None),
        P(("grp", "ep"), None),
        P("ep", None, "tp"),
        P("ep", None, "tp"),
        P("ep", None, "tp"),
        P("ep", None, "tp"),
        P("ep", None, "tp"),
        P("ep", None, "tp"),
        P("ep", None, "tp"),
        P("ep", None, "tp"),
        P("ep", None, "tp"),
    )
    out_specs = P(("grp", "ep"), "tp")
    experts = mesh.shape["ep"]
    few = mesh.shape["tp"] == 1 and experts == 16
    return jax.shard_map(
        dense if few else routed,
        mesh=mesh,
        in_specs=in_specs,
        out_specs=out_specs,
        check_vma=False,
    )
```

```python
import functools

import jax
import jax.numpy as jnp
from jax import lax
from jax.experimental import pallas as pl
from jax.experimental.pallas import tpu as pltpu
from jax.sharding import PartitionSpec as P

route_scale = 2.5
GROUP = 128
WORD = 4
CHUNK = GROUP * WORD
EXTRA = 128
QUARTERS = 4
F32 = jnp.float32
BF16 = jnp.bfloat16


def dequantize(words, scales, zeros):
    groups = scales.shape[0]
    packed = words.reshape(groups, words.shape[0] // groups, 1, words.shape[1])
    powers = jnp.array([1.0, 16.0, 256.0, 4096.0], jnp.float32)[None, None, :, None]
    lower = jnp.floor(packed / powers)
    higher = jnp.floor(packed / (16.0 * powers))
    codes = lower - 16.0 * higher
    values = (codes - zeros.astype(jnp.float32)[:, None, None, :]) * scales.astype(jnp.float32)[
        :, None, None, :
    ]
    return values.reshape(-1, words.shape[1]).astype(jnp.bfloat16)


def routed(
    tokens,
    gate_scores,
    route_ids,
    gate_codes,
    up_codes,
    down_codes,
    gate_scale,
    up_scale,
    down_scale,
    gate_zero,
    up_zero,
    down_zero,
):
    experts = lax.axis_size("ep")
    tok_rows, half_width = tokens.shape
    topk = route_ids.shape[1]
    capacity = min(tok_rows, max(2, 5 * tok_rows * topk // (4 * experts)))
    w_gate = dequantize(gate_codes[0], gate_scale[0], gate_zero[0])
    w_up = dequantize(up_codes[0], up_scale[0], up_zero[0])
    w_down = dequantize(down_codes[0], down_scale[0], down_zero[0])
    flat_ids = route_ids.reshape(-1)
    onehot = (flat_ids[:, None] == jnp.arange(experts, dtype=jnp.int32)[None, :]).astype(jnp.int32)
    earlier = jnp.cumsum(onehot, axis=0) - onehot
    slot = jnp.sum(earlier * onehot, axis=1)
    target = (flat_ids * capacity + slot).reshape(tok_rows, topk)
    places = jnp.arange(experts * capacity, dtype=jnp.int32)
    selector = jnp.sum(
        (places[:, None, None] == target[None, :, :]).astype(jnp.float32), axis=2
    ).astype(jnp.bfloat16)
    outgoing = jnp.dot(selector, tokens, preferred_element_type=jnp.float32).astype(jnp.bfloat16)
    outgoing = outgoing.reshape(experts, capacity, half_width)
    whole = lax.all_gather(
        lax.all_to_all(outgoing, "ep", split_axis=0, concat_axis=0, tiled=True),
        "tp",
        axis=2,
        tiled=True,
    )
    count = whole.shape[1]
    flat_rows = whole.reshape(-1, whole.shape[2])
    gate = jnp.dot(flat_rows, w_gate, preferred_element_type=jnp.float32)
    up = jnp.dot(flat_rows, w_up, preferred_element_type=jnp.float32)
    hidden = (jax.nn.silu(gate) * up).astype(jnp.bfloat16)
    summed = jnp.dot(
        lax.all_gather(hidden, "tp", axis=1, tiled=True), w_down, preferred_element_type=jnp.float32
    )
    answer = summed.astype(jnp.bfloat16).reshape(experts, count, w_down.shape[1])
    returned = lax.all_to_all(answer, "ep", split_axis=0, concat_axis=0, tiled=True)
    weights = route_scale * gate_scores / jnp.sum(gate_scores, axis=1, keepdims=True)
    weighting = jnp.sum(
        jnp.where(places[None, None, :] == target[:, :, None], weights[:, :, None], 0.0), axis=1
    )
    answers = returned.reshape(experts * capacity, half_width).astype(jnp.float32)
    combined = jnp.dot(weighting, answers, precision=lax.Precision.HIGHEST)
    return combined.astype(jnp.bfloat16)


def prepare_kernel(
    experts, mine, all_tokens, all_scores, all_ids, rows, perm, index, tokens, scores, ids, arrived
):
    index[0] = mine[0]
    fetches = [
        pltpu.make_async_copy(source, held, arrived.at[i])
        for i, (source, held) in enumerate(
            ((all_tokens, tokens), (all_scores, scores), (all_ids, ids))
        )
    ]
    for fetch in fetches:
        fetch.start()
    source = lax.broadcasted_iota(jnp.int32, (CHUNK, CHUNK), 0)
    place = lax.broadcasted_iota(jnp.int32, (CHUNK, CHUNK), 1)
    perm[...] = jnp.where((source & 3) * GROUP + (source >> 2) == place, 1.0, 0.0).astype(BF16)
    width = tokens.shape[1]
    for fetch in fetches:
        fetch.wait()
    for at in range(0, width, CHUNK):
        rows[:, at : at + CHUNK] = jnp.dot(
            tokens[:, at : at + CHUNK], perm[...], preferred_element_type=F32
        ).astype(BF16)
    weights = route_scale * scores[...] / jnp.sum(scores[...], axis=0, keepdims=True)
    n = tokens.shape[0]
    lane = lax.broadcasted_iota(jnp.int32, (EXTRA, n), 0)
    spread = jnp.zeros((EXTRA, n), F32)
    for k in range(ids.shape[0]):
        spread += jnp.where(lane % experts == ids[k : k + 1, :], weights[k : k + 1, :], 0.0)
    high = spread.astype(BF16).astype(F32)
    mid = (spread - high).astype(BF16).astype(F32)
    low = spread - high - mid
    part = lane // experts
    spread = jnp.where(
        part == 0, high, jnp.where(part == 1, mid, jnp.where(part == 2, low, 0.0))
    )
    square = jnp.concatenate([spread, jnp.zeros((EXTRA, EXTRA - n), F32)], axis=1)
    rows[:, width:] = square.T[:n].astype(BF16)


def prepare(mine, tokens, scores, ids, experts):
    n, width = tokens.shape
    smem, vmem = pl.BlockSpec(memory_space=pltpu.SMEM), pl.BlockSpec(memory_space=pltpu.VMEM)
    return pl.pallas_call(
        functools.partial(prepare_kernel, experts),
        out_shape=(
            jax.ShapeDtypeStruct((n, width + EXTRA), BF16),
            jax.ShapeDtypeStruct((CHUNK, CHUNK), BF16),
            jax.ShapeDtypeStruct((1,), jnp.int32),
        ),
        in_specs=[smem] + [pl.BlockSpec(memory_space=pl.ANY)] * 3,
        out_specs=(vmem, vmem, smem),
        scratch_shapes=[
            pltpu.VMEM(tokens.shape, BF16),
            pltpu.VMEM(scores.shape[::-1], F32),
            pltpu.VMEM(ids.shape[::-1], jnp.int32),
            pltpu.SemaphoreType.DMA((3,)),
        ],
        compiler_params=pltpu.CompilerParams(vmem_limit_bytes=8 * 1024 * 1024),
        name="prepare",
    )(mine, *[pltpu.with_memory_space_constraint(a, pltpu.HBM) for a in (tokens, scores.T, ids.T)])


def unpack_kernel(later, words, scale, zero, *refs):
    out, done, scales, zeros, held, arrived = refs[later:]
    at = pl.program_id(0)
    sub = GROUP // WORD
    tiles, _, tile = out.shape

    def fetch(i):
        rows = slice(i * GROUP, (i + 1) * GROUP)
        return pltpu.make_async_copy(words.at[rows], held.at[i], arrived.at[i])

    @pl.when(at == 0)
    def _():
        for i in range(held.shape[0]):
            fetch(i).start()
        scales[...] = scale[...].astype(F32)
        zeros[...] = zero[...].astype(F32)
        done[...] = jnp.zeros(done.shape, F32)

    for i in range(held.shape[0]):

        @pl.when(at == i)
        def _():
            fetch(i).wait()

    for t in range(tiles):
        cols = slice(t * tile, (t + 1) * tile)
        for g in range(WORD):
            s = scales[pl.ds(at * WORD + g, 1), cols]
            z = zeros[pl.ds(at * WORD + g, 1), cols]
            w = held[at, g * sub : (g + 1) * sub, cols].astype(jnp.int32)
            for j in range(WORD):
                code = ((w >> (4 * j)) & 15).astype(F32)
                begin = pl.multiple_of(at * CHUNK + j * GROUP + g * sub, sub)
                out[t, pl.ds(begin, sub), :] = ((code - z) * s).astype(BF16)


def unpack(words, scale, zero, tile, before=()):
    n, cols = words.shape
    tiles, steps = cols // tile, n // GROUP
    words = pltpu.with_memory_space_constraint(words, pltpu.HBM)
    resident = pl.BlockSpec(memory_space=pltpu.VMEM)
    return pl.pallas_call(
        functools.partial(unpack_kernel, len(before)),
        grid=(steps,),
        in_specs=[pl.BlockSpec(memory_space=pl.ANY)] + [resident] * (2 + len(before)),
        out_specs=[resident] * 2,
        out_shape=[
            pltpu.VMEM((tiles, n * WORD, tile), BF16),
            jax.ShapeDtypeStruct((8, 128), F32),
        ],
        scratch_shapes=[
            pltpu.VMEM(scale.shape, F32),
            pltpu.VMEM(zero.shape, F32),
            pltpu.VMEM((steps, GROUP, cols), F32),
            pltpu.SemaphoreType.DMA((steps,)),
        ],
        compiler_params=pltpu.CompilerParams(vmem_limit_bytes=14 * 1024 * 1024),
        cost_estimate=pl.CostEstimate(
            flops=n * cols * 24, bytes_accessed=n * cols * 4, transcendentals=0
        ),
        name="unpack",
    )(words, scale, zero, *before)


def pack_kernel(cuts, *refs):
    out = refs[-1]
    at = 0
    for ref, (begin, count) in zip(refs, cuts):
        out[at : at + count, :] = ref[begin : begin + count, :]
        at += count


def pack(pieces, before=()):
    resident = pl.BlockSpec(memory_space=pltpu.VMEM)
    cuts = [(begin, count) for _, begin, count in pieces]
    rows = sum(count for _, count in cuts)
    return pl.pallas_call(
        functools.partial(pack_kernel, cuts),
        in_specs=[resident] * (len(pieces) + len(before)),
        out_specs=resident,
        out_shape=jax.ShapeDtypeStruct((rows, pieces[0][0].shape[1]), BF16),
        compiler_params=pltpu.CompilerParams(vmem_limit_bytes=4 * 1024 * 1024),
        cost_estimate=pl.CostEstimate(flops=0, bytes_accessed=rows * 4096, transcendentals=0),
        name="pack",
    )(*[p for p, _, _ in pieces], *before)


def join_kernel(parts, *refs):
    own, crossing = refs[-2:]
    half = own.shape[0] // parts
    for p in range(parts):
        keep, got = refs[2 * p], refs[2 * p + 1]
        rows = slice(p * half, (p + 1) * half)
        own[rows, :] = keep[:half].astype(F32) + got[:half].astype(F32)
        crossing[rows, :] = (keep[half:].astype(F32) + got[half:].astype(F32)).astype(BF16)


def join(keeps, gots, before=()):
    resident = pl.BlockSpec(memory_space=pltpu.VMEM)
    rows, width = keeps[0].shape
    parts = len(keeps)
    pairs = [a for pair in zip(keeps, gots) for a in pair]
    return pl.pallas_call(
        functools.partial(join_kernel, parts),
        in_specs=[resident] * (len(pairs) + len(before)),
        out_specs=[resident] * 2,
        out_shape=[
            jax.ShapeDtypeStruct((parts * rows // 2, width), F32),
            jax.ShapeDtypeStruct((parts * rows // 2, width), BF16),
        ],
        compiler_params=pltpu.CompilerParams(vmem_limit_bytes=4 * 1024 * 1024),
        cost_estimate=pl.CostEstimate(flops=0, bytes_accessed=rows * 4096, transcendentals=0),
        name="join",
    )(*pairs, *before)


def land_kernel(parts, own, got, *refs):
    leaving, staying = refs[-2:]
    u = staying.shape[0] // parts
    for p in range(parts):
        sums = []
        for k in range(3):
            rows = slice((3 * p + k) * u, (3 * p + k + 1) * u)
            sums.append(own[rows].astype(F32) + got[rows].astype(F32))
        leaving[p * u : (p + 1) * u, :] = sums[0].astype(BF16)
        leaving[(parts + p) * u : (parts + p + 1) * u, :] = sums[2].astype(BF16)
        staying[p * u : (p + 1) * u, :] = sums[1]


def land(own, got, parts, before=()):
    resident = pl.BlockSpec(memory_space=pltpu.VMEM)
    rows, width = own.shape
    return pl.pallas_call(
        functools.partial(land_kernel, parts),
        in_specs=[resident] * (2 + len(before)),
        out_specs=[resident] * 2,
        out_shape=[
            jax.ShapeDtypeStruct((2 * rows // 3, width), BF16),
            jax.ShapeDtypeStruct((rows // 3, width), F32),
        ],
        compiler_params=pltpu.CompilerParams(vmem_limit_bytes=4 * 1024 * 1024),
        cost_estimate=pl.CostEstimate(flops=0, bytes_accessed=rows * 4096, transcendentals=0),
        name="land",
    )(own, got, *before)


def pass_kernel(staying, got, *refs):
    u = staying.shape[0]
    refs[-1][...] = (staying[...] + got[u:].astype(F32)).astype(BF16)


def pass_on(staying, got, before=()):
    resident = pl.BlockSpec(memory_space=pltpu.VMEM)
    return pl.pallas_call(
        pass_kernel,
        in_specs=[resident] * (2 + len(before)),
        out_specs=resident,
        out_shape=jax.ShapeDtypeStruct(staying.shape, BF16),
        compiler_params=pltpu.CompilerParams(vmem_limit_bytes=4 * 1024 * 1024),
        cost_estimate=pl.CostEstimate(
            flops=0, bytes_accessed=staying.shape[0] * 4096, transcendentals=0
        ),
        name="pass_on",
    )(staying, got, *before)


def expert_kernel(
    experts, quarter, later, mine, near, cross, other, z, x, c, perm, wg, wu, wd, *refs
):
    keep_near, keep_far, send_near, send_far, done, xs, hs, hp = refs[later:]
    n, width = near.shape[0], near.shape[1] - EXTRA
    far = z.shape[0]
    u = far // 3
    tiles, _, tile = wg.shape

    done[...] = jnp.zeros(done.shape, F32)
    mine_at = quarter * u
    weights = []
    at = 0
    for ref, begin, count in (
        (near, mine_at, u),
        (cross, mine_at, u),
        (z, 0, far),
        (x, 0, far),
        (other, mine_at, u),
        (other, n + mine_at, u),
        (c, 0, 2 * far),
    ):
        xs[at : at + count, :] = ref[begin : begin + count, :width]
        parts = ref[begin : begin + count, width:].astype(F32)
        lane = lax.broadcasted_iota(jnp.int32, parts.shape, 1)
        parts = jnp.where(lane % experts == mine[0], parts, 0.0)
        weights.append(jnp.sum(parts, axis=1, keepdims=True))
        at += count
    weights = jnp.concatenate(weights, axis=0)

    for t in range(tiles):
        gate = jnp.dot(xs[...], wg[t], preferred_element_type=F32)
        up = jnp.dot(xs[...], wu[t], preferred_element_type=F32)
        hs[:, t * tile : (t + 1) * tile] = (gate / (1.0 + jnp.exp(-gate)) * up).astype(BF16)
    for begin in range(0, hs.shape[1], CHUNK):
        cols = slice(begin, begin + CHUNK)
        hp[:, cols] = jnp.dot(hs[:, cols], perm[...], preferred_element_type=F32).astype(BF16)
    for t in range(wd.shape[0]):
        cols = slice(t * wd.shape[2], (t + 1) * wd.shape[2])
        answer = (jnp.dot(hp[...], wd[t], preferred_element_type=F32) * weights).astype(BF16)
        at = 0
        for ref in (keep_near, keep_far, send_near, send_far):
            ref[:, cols] = answer[at : at + ref.shape[0]]
            at += ref.shape[0]


def expert_block(quarter, mine, near, cross, other, z, x, c, perm, wg, wu, wd, experts, before):
    far, wide = z.shape
    u = far // 3
    width = wide - EXTRA
    hidden = wd.shape[1]
    rows = 16 * u
    resident = pl.BlockSpec(memory_space=pltpu.VMEM)
    return pl.pallas_call(
        functools.partial(expert_kernel, experts, quarter, len(before)),
        in_specs=[pl.BlockSpec(memory_space=pltpu.SMEM)] + [resident] * (10 + len(before)),
        out_specs=[resident] * 5,
        out_shape=[jax.ShapeDtypeStruct((n * u, width), BF16) for n in (2, 6, 2, 6)]
        + [jax.ShapeDtypeStruct((8, 128), F32)],
        scratch_shapes=[
            pltpu.VMEM((rows, width), BF16),
            pltpu.VMEM((rows, hidden), BF16),
            pltpu.VMEM((rows, hidden), BF16),
        ],
        compiler_params=pltpu.CompilerParams(vmem_limit_bytes=14 * 1024 * 1024),
        cost_estimate=pl.CostEstimate(
            flops=2 * rows * width * hidden * 3,
            bytes_accessed=rows * width * 4,
            transcendentals=rows * hidden,
        ),
        name="expert_block",
    )(mine, near, cross, other, z, x, c, perm, wg, wu, wd, *before)


def dense(
    tokens,
    gate_scores,
    route_ids,
    gate_codes,
    up_codes,
    down_codes,
    gate_scale,
    up_scale,
    down_scale,
    gate_zero,
    up_zero,
    down_zero,
):
    experts = lax.axis_size("ep")
    n = tokens.shape[0]
    u = n // QUARTERS
    mine = lax.axis_index("ep").astype(jnp.int32).reshape(1)

    def swap(value, bits):
        return lax.ppermute(value, "ep", [(i, i ^ bits) for i in range(experts)])

    quarters = range(QUARTERS)
    rows, perm, mine = prepare(mine, tokens, gate_scores, route_ids, experts)

    half = n // 2
    cross = swap(rows, 2)
    first = [swap(rows[:half], 4 * k) for k in range(1, 4)]
    w_down, done_down = unpack(down_codes[0], down_scale[0], down_zero[0], 1792)
    w_gate, done_gate = unpack(gate_codes[0], gate_scale[0], gate_zero[0], 512)
    w_up, done_up = unpack(up_codes[0], up_scale[0], up_zero[0], 512)
    unpacked = [done_down, done_gate, done_up]

    z = [pack([(first[k], q * u, u) for k in range(3)], unpacked) for q in range(2)]
    two = swap(pack([(rows, half, half)], z), 8)
    onward = pack([(rows, half, half), (two, 0, half)], unpacked)
    one = swap(onward, 4)
    other = swap(pack([(rows, 0, n), (cross, 0, n)], unpacked), 1)
    two_x = swap(pack([(cross, 3 * u, u)], unpacked), 8)
    x = [swap(v, 2) for v in z]
    done, near, far, sent = [], [], [], []

    def expert(q, ahead, before):
        both = pack([(z[q], 0, 3 * u), (x[q], 0, 3 * u)], done[-1:] + ahead)
        keep_near, keep_far, send_near, send_far, token = expert_block(
            q, mine, rows, cross, other, z[q], x[q], swap(both, 1), perm,
            w_gate, w_up, w_down, experts, before,
        )
        done.append(token)
        near.append((keep_near, send_near))
        far.append(keep_far)
        sent.append(send_far)

    def after_core(q, before):
        own, crossing = join([far[q]], [swap(sent[q], 1)], before)
        return own, crossing, swap(crossing, 2)

    expert(0, [onward], [])
    z += [
        pack([(one, q * u, u), (two, q * u, u), (one, half + q * u, u)], done[-1:])
        for q in range(2)
    ]
    x.append(swap(z[2], 2))
    onward_x = pack([(cross, 3 * u, u), (two_x, 0, u)], done[-1:])
    one_x = swap(onward_x, 4)
    leaving_0, staying_0 = land(far[0], swap(sent[0], 1), 2, done[-1:])
    expert(1, [onward_x, z[2], z[3]], [leaving_0])
    x.append(pack([(one_x, 0, u), (two_x, 0, u), (one_x, u, u)], done[-1:]))
    own_1, crossing_1, crossed_1 = after_core(1, done[-1:])
    expert(2, [x[3]], [crossing_1])
    got_0 = swap(leaving_0, 4)
    passed_0 = pass_on(staying_0, got_0, done[-1:])
    leaving_1, staying_1 = land(own_1, crossed_1, 1, done[-1:])
    own_2, crossing_2, crossed_2 = after_core(2, done[-1:])
    expert(3, [passed_0, leaving_1], [crossing_2])
    got_1 = swap(leaving_1, 4)
    passed_1 = pass_on(staying_1, got_1, done[-1:])
    leaving_2, staying_2 = land(own_2, crossed_2, 1, done[-1:])
    sent[3] = pack([(sent[3], 0, 6 * u)], [passed_1, leaving_2])
    own_3, crossing_3, crossed_3 = after_core(3, done[-1:])
    leaving_3, staying_3 = land(own_3, crossed_3, 1)

    sends = [s for _, s in near]
    kept = [k for k, _ in near]
    send = pack([(s, 0, u) for s in sends] + [(s, u, u) for s in sends], done[-1:])
    keep = pack([(k, 0, u) for k in kept] + [(k, u, u) for k in kept], done[-1:])
    last_0 = swap(passed_0, 8)
    sum_0 = got_0[: 2 * u].astype(F32) + last_0.astype(F32)
    pair = keep.astype(F32) + swap(send, 1).astype(F32)
    away = jnp.concatenate([pair[n : n + u] + sum_0[u:], pair[n + u :]]).astype(BF16)
    over = [swap(away[:half], 2), swap(away[half:], 2)]
    got_2, got_3 = swap(leaving_2, 4), swap(leaving_3, 4)
    passed_2 = pass_on(staying_2, got_2, [crossing_3])
    passed_3 = pass_on(staying_3, got_3, [over[0]])
    sums = [sum_0[:u]]
    for got, passed in ((got_1, passed_1), (got_2, passed_2), (got_3, passed_3)):
        sums.append(got[:u].astype(F32) + swap(passed, 8).astype(F32))
    total = pair[:n] + jnp.concatenate(over).astype(F32) + jnp.concatenate(sums)
    return total.astype(BF16)


def solution(mesh):
    in_specs = (
        P(("grp", "ep"), "tp"),
        P(("grp", "ep"), None),
        P(("grp", "ep"), None),
        P("ep", None, "tp"),
        P("ep", None, "tp"),
        P("ep", None, "tp"),
        P("ep", None, "tp"),
        P("ep", None, "tp"),
        P("ep", None, "tp"),
        P("ep", None, "tp"),
        P("ep", None, "tp"),
        P("ep", None, "tp"),
    )
    out_specs = P(("grp", "ep"), "tp")
    experts = mesh.shape["ep"]
    few = mesh.shape["tp"] == 1 and experts == 16
    return jax.shard_map(
        dense if few else routed,
        mesh=mesh,
        in_specs=in_specs,
        out_specs=out_specs,
        check_vma=False,
    )
```

```python
import functools

import jax
import jax.numpy as jnp
from jax import lax
from jax.experimental import pallas as pl
from jax.experimental.pallas import tpu as pltpu
from jax.sharding import PartitionSpec as P

route_scale = 2.5
GROUP = 128
WORD = 4
CHUNK = GROUP * WORD
EXTRA = 128
QUARTERS = 4
F32 = jnp.float32
BF16 = jnp.bfloat16


def dequantize(words, scales, zeros):
    groups = scales.shape[0]
    packed = words.reshape(groups, words.shape[0] // groups, 1, words.shape[1])
    powers = jnp.array([1.0, 16.0, 256.0, 4096.0], jnp.float32)[None, None, :, None]
    lower = jnp.floor(packed / powers)
    higher = jnp.floor(packed / (16.0 * powers))
    codes = lower - 16.0 * higher
    values = (codes - zeros.astype(jnp.float32)[:, None, None, :]) * scales.astype(jnp.float32)[
        :, None, None, :
    ]
    return values.reshape(-1, words.shape[1]).astype(jnp.bfloat16)


def routed(
    tokens,
    gate_scores,
    route_ids,
    gate_codes,
    up_codes,
    down_codes,
    gate_scale,
    up_scale,
    down_scale,
    gate_zero,
    up_zero,
    down_zero,
):
    experts = lax.axis_size("ep")
    tok_rows, half_width = tokens.shape
    topk = route_ids.shape[1]
    capacity = min(tok_rows, max(2, 5 * tok_rows * topk // (4 * experts)))
    w_gate = dequantize(gate_codes[0], gate_scale[0], gate_zero[0])
    w_up = dequantize(up_codes[0], up_scale[0], up_zero[0])
    w_down = dequantize(down_codes[0], down_scale[0], down_zero[0])
    flat_ids = route_ids.reshape(-1)
    onehot = (flat_ids[:, None] == jnp.arange(experts, dtype=jnp.int32)[None, :]).astype(jnp.int32)
    earlier = jnp.cumsum(onehot, axis=0) - onehot
    slot = jnp.sum(earlier * onehot, axis=1)
    target = (flat_ids * capacity + slot).reshape(tok_rows, topk)
    places = jnp.arange(experts * capacity, dtype=jnp.int32)
    selector = jnp.sum(
        (places[:, None, None] == target[None, :, :]).astype(jnp.float32), axis=2
    ).astype(jnp.bfloat16)
    outgoing = jnp.dot(selector, tokens, preferred_element_type=jnp.float32).astype(jnp.bfloat16)
    outgoing = outgoing.reshape(experts, capacity, half_width)
    whole = lax.all_gather(
        lax.all_to_all(outgoing, "ep", split_axis=0, concat_axis=0, tiled=True),
        "tp",
        axis=2,
        tiled=True,
    )
    count = whole.shape[1]
    flat_rows = whole.reshape(-1, whole.shape[2])
    gate = jnp.dot(flat_rows, w_gate, preferred_element_type=jnp.float32)
    up = jnp.dot(flat_rows, w_up, preferred_element_type=jnp.float32)
    hidden = (jax.nn.silu(gate) * up).astype(jnp.bfloat16)
    summed = jnp.dot(
        lax.all_gather(hidden, "tp", axis=1, tiled=True), w_down, preferred_element_type=jnp.float32
    )
    answer = summed.astype(jnp.bfloat16).reshape(experts, count, w_down.shape[1])
    returned = lax.all_to_all(answer, "ep", split_axis=0, concat_axis=0, tiled=True)
    weights = route_scale * gate_scores / jnp.sum(gate_scores, axis=1, keepdims=True)
    weighting = jnp.sum(
        jnp.where(places[None, None, :] == target[:, :, None], weights[:, :, None], 0.0), axis=1
    )
    answers = returned.reshape(experts * capacity, half_width).astype(jnp.float32)
    combined = jnp.dot(weighting, answers, precision=lax.Precision.HIGHEST)
    return combined.astype(jnp.bfloat16)


def prepare_kernel(
    experts, mine, all_tokens, all_scores, all_ids, rows, perm, index, tokens, scores, ids, arrived
):
    index[0] = mine[0]
    fetches = [
        pltpu.make_async_copy(source, held, arrived.at[i])
        for i, (source, held) in enumerate(
            ((all_tokens, tokens), (all_scores, scores), (all_ids, ids))
        )
    ]
    for fetch in fetches:
        fetch.start()
    source = lax.broadcasted_iota(jnp.int32, (CHUNK, CHUNK), 0)
    place = lax.broadcasted_iota(jnp.int32, (CHUNK, CHUNK), 1)
    perm[...] = jnp.where((source & 3) * GROUP + (source >> 2) == place, 1.0, 0.0).astype(BF16)
    width = tokens.shape[1]
    for fetch in fetches:
        fetch.wait()
    for at in range(0, width, CHUNK):
        rows[:, at : at + CHUNK] = jnp.dot(
            tokens[:, at : at + CHUNK], perm[...], preferred_element_type=F32
        ).astype(BF16)
    weights = route_scale * scores[...] / jnp.sum(scores[...], axis=0, keepdims=True)
    n = tokens.shape[0]
    lane = lax.broadcasted_iota(jnp.int32, (EXTRA, n), 0)
    spread = jnp.zeros((EXTRA, n), F32)
    for k in range(ids.shape[0]):
        spread += jnp.where(lane % experts == ids[k : k + 1, :], weights[k : k + 1, :], 0.0)
    high = spread.astype(BF16).astype(F32)
    mid = (spread - high).astype(BF16).astype(F32)
    low = spread - high - mid
    part = lane // experts
    spread = jnp.where(
        part == 0, high, jnp.where(part == 1, mid, jnp.where(part == 2, low, 0.0))
    )
    square = jnp.concatenate([spread, jnp.zeros((EXTRA, EXTRA - n), F32)], axis=1)
    rows[:, width:] = square.T[:n].astype(BF16)


def prepare(mine, tokens, scores, ids, experts):
    n, width = tokens.shape
    smem, vmem = pl.BlockSpec(memory_space=pltpu.SMEM), pl.BlockSpec(memory_space=pltpu.VMEM)
    return pl.pallas_call(
        functools.partial(prepare_kernel, experts),
        out_shape=(
            jax.ShapeDtypeStruct((n, width + EXTRA), BF16),
            jax.ShapeDtypeStruct((CHUNK, CHUNK), BF16),
            jax.ShapeDtypeStruct((1,), jnp.int32),
        ),
        in_specs=[smem] + [pl.BlockSpec(memory_space=pl.ANY)] * 3,
        out_specs=(vmem, vmem, smem),
        scratch_shapes=[
            pltpu.VMEM(tokens.shape, BF16),
            pltpu.VMEM(scores.shape[::-1], F32),
            pltpu.VMEM(ids.shape[::-1], jnp.int32),
            pltpu.SemaphoreType.DMA((3,)),
        ],
        compiler_params=pltpu.CompilerParams(vmem_limit_bytes=8 * 1024 * 1024),
        name="prepare",
    )(mine, *[pltpu.with_memory_space_constraint(a, pltpu.HBM) for a in (tokens, scores.T, ids.T)])


def unpack_kernel(later, words, scale, zero, *refs):
    out, done, scales, zeros, held, arrived = refs[later:]
    at = pl.program_id(0)
    sub = GROUP // WORD
    tiles, _, tile = out.shape

    def fetch(i):
        rows = slice(i * GROUP, (i + 1) * GROUP)
        return pltpu.make_async_copy(words.at[rows], held.at[i], arrived.at[i])

    @pl.when(at == 0)
    def _():
        for i in range(held.shape[0]):
            fetch(i).start()
        scales[...] = scale[...].astype(F32)
        zeros[...] = zero[...].astype(F32)
        done[...] = jnp.zeros(done.shape, F32)

    for i in range(held.shape[0]):

        @pl.when(at == i)
        def _():
            fetch(i).wait()

    for t in range(tiles):
        cols = slice(t * tile, (t + 1) * tile)
        for g in range(WORD):
            s = scales[pl.ds(at * WORD + g, 1), cols]
            z = zeros[pl.ds(at * WORD + g, 1), cols]
            w = held[at, g * sub : (g + 1) * sub, cols].astype(jnp.int32)
            for j in range(WORD):
                code = ((w >> (4 * j)) & 15).astype(F32)
                begin = pl.multiple_of(at * CHUNK + j * GROUP + g * sub, sub)
                out[t, pl.ds(begin, sub), :] = ((code - z) * s).astype(BF16)


def unpack(words, scale, zero, tile, before=()):
    n, cols = words.shape
    tiles, steps = cols // tile, n // GROUP
    words = pltpu.with_memory_space_constraint(words, pltpu.HBM)
    resident = pl.BlockSpec(memory_space=pltpu.VMEM)
    return pl.pallas_call(
        functools.partial(unpack_kernel, len(before)),
        grid=(steps,),
        in_specs=[pl.BlockSpec(memory_space=pl.ANY)] + [resident] * (2 + len(before)),
        out_specs=[resident] * 2,
        out_shape=[
            pltpu.VMEM((tiles, n * WORD, tile), BF16),
            jax.ShapeDtypeStruct((8, 128), F32),
        ],
        scratch_shapes=[
            pltpu.VMEM(scale.shape, F32),
            pltpu.VMEM(zero.shape, F32),
            pltpu.VMEM((steps, GROUP, cols), F32),
            pltpu.SemaphoreType.DMA((steps,)),
        ],
        compiler_params=pltpu.CompilerParams(vmem_limit_bytes=14 * 1024 * 1024),
        cost_estimate=pl.CostEstimate(
            flops=n * cols * 24, bytes_accessed=n * cols * 4, transcendentals=0
        ),
        name="unpack",
    )(words, scale, zero, *before)


def pack_kernel(cuts, *refs):
    out = refs[-1]
    at = 0
    for ref, (begin, count) in zip(refs, cuts):
        out[at : at + count, :] = ref[begin : begin + count, :]
        at += count


def pack(pieces, before=()):
    resident = pl.BlockSpec(memory_space=pltpu.VMEM)
    cuts = [(begin, count) for _, begin, count in pieces]
    rows = sum(count for _, count in cuts)
    return pl.pallas_call(
        functools.partial(pack_kernel, cuts),
        in_specs=[resident] * (len(pieces) + len(before)),
        out_specs=resident,
        out_shape=jax.ShapeDtypeStruct((rows, pieces[0][0].shape[1]), BF16),
        compiler_params=pltpu.CompilerParams(vmem_limit_bytes=4 * 1024 * 1024),
        cost_estimate=pl.CostEstimate(flops=0, bytes_accessed=rows * 4096, transcendentals=0),
        name="pack",
    )(*[p for p, _, _ in pieces], *before)


def join_kernel(parts, *refs):
    own, crossing = refs[-2:]
    half = own.shape[0] // parts
    for p in range(parts):
        keep, got = refs[2 * p], refs[2 * p + 1]
        rows = slice(p * half, (p + 1) * half)
        own[rows, :] = keep[:half].astype(F32) + got[:half].astype(F32)
        crossing[rows, :] = (keep[half:].astype(F32) + got[half:].astype(F32)).astype(BF16)


def join(keeps, gots, before=()):
    resident = pl.BlockSpec(memory_space=pltpu.VMEM)
    rows, width = keeps[0].shape
    parts = len(keeps)
    pairs = [a for pair in zip(keeps, gots) for a in pair]
    return pl.pallas_call(
        functools.partial(join_kernel, parts),
        in_specs=[resident] * (len(pairs) + len(before)),
        out_specs=[resident] * 2,
        out_shape=[
            jax.ShapeDtypeStruct((parts * rows // 2, width), F32),
            jax.ShapeDtypeStruct((parts * rows // 2, width), BF16),
        ],
        compiler_params=pltpu.CompilerParams(vmem_limit_bytes=4 * 1024 * 1024),
        cost_estimate=pl.CostEstimate(flops=0, bytes_accessed=rows * 4096, transcendentals=0),
        name="join",
    )(*pairs, *before)


def land_kernel(parts, own, got, *refs):
    leaving, staying = refs[-2:]
    u = staying.shape[0] // parts
    for p in range(parts):
        sums = []
        for k in range(3):
            rows = slice((3 * p + k) * u, (3 * p + k + 1) * u)
            sums.append(own[rows].astype(F32) + got[rows].astype(F32))
        leaving[p * u : (p + 1) * u, :] = sums[0].astype(BF16)
        leaving[(parts + p) * u : (parts + p + 1) * u, :] = sums[2].astype(BF16)
        staying[p * u : (p + 1) * u, :] = sums[1]


def land(own, got, parts, before=()):
    resident = pl.BlockSpec(memory_space=pltpu.VMEM)
    rows, width = own.shape
    return pl.pallas_call(
        functools.partial(land_kernel, parts),
        in_specs=[resident] * (2 + len(before)),
        out_specs=[resident] * 2,
        out_shape=[
            jax.ShapeDtypeStruct((2 * rows // 3, width), BF16),
            jax.ShapeDtypeStruct((rows // 3, width), F32),
        ],
        compiler_params=pltpu.CompilerParams(vmem_limit_bytes=4 * 1024 * 1024),
        cost_estimate=pl.CostEstimate(flops=0, bytes_accessed=rows * 4096, transcendentals=0),
        name="land",
    )(own, got, *before)


def pass_kernel(staying, got, *refs):
    u = staying.shape[0]
    refs[-1][...] = (staying[...] + got[u:].astype(F32)).astype(BF16)


def pass_on(staying, got, before=()):
    resident = pl.BlockSpec(memory_space=pltpu.VMEM)
    return pl.pallas_call(
        pass_kernel,
        in_specs=[resident] * (2 + len(before)),
        out_specs=resident,
        out_shape=jax.ShapeDtypeStruct(staying.shape, BF16),
        compiler_params=pltpu.CompilerParams(vmem_limit_bytes=4 * 1024 * 1024),
        cost_estimate=pl.CostEstimate(
            flops=0, bytes_accessed=staying.shape[0] * 4096, transcendentals=0
        ),
        name="pass_on",
    )(staying, got, *before)


def expert_kernel(
    experts, quarter, later, mine, near, cross, other, z, x, c, perm, wg, wu, wd, *refs
):
    keep_near, keep_far, send_near, send_far, done, xs, hs, hp = refs[later:]
    n, width = near.shape[0], near.shape[1] - EXTRA
    far = z.shape[0]
    u = far // 3
    tiles, _, tile = wg.shape

    done[...] = jnp.zeros(done.shape, F32)
    mine_at = quarter * u
    weights = []
    at = 0
    for ref, begin, count in (
        (near, mine_at, u),
        (cross, mine_at, u),
        (z, 0, far),
        (x, 0, far),
        (other, mine_at, u),
        (other, n + mine_at, u),
        (c, 0, 2 * far),
    ):
        xs[at : at + count, :] = ref[begin : begin + count, :width]
        parts = ref[begin : begin + count, width:].astype(F32)
        lane = lax.broadcasted_iota(jnp.int32, parts.shape, 1)
        parts = jnp.where(lane % experts == mine[0], parts, 0.0)
        weights.append(jnp.sum(parts, axis=1, keepdims=True))
        at += count
    weights = jnp.concatenate(weights, axis=0)

    for t in range(tiles):
        gate = jnp.dot(xs[...], wg[t], preferred_element_type=F32)
        up = jnp.dot(xs[...], wu[t], preferred_element_type=F32)
        hs[:, t * tile : (t + 1) * tile] = (gate / (1.0 + jnp.exp(-gate)) * up).astype(BF16)
    for begin in range(0, hs.shape[1], CHUNK):
        cols = slice(begin, begin + CHUNK)
        hp[:, cols] = jnp.dot(hs[:, cols], perm[...], preferred_element_type=F32).astype(BF16)
    for t in range(wd.shape[0]):
        cols = slice(t * wd.shape[2], (t + 1) * wd.shape[2])
        answer = (jnp.dot(hp[...], wd[t], preferred_element_type=F32) * weights).astype(BF16)
        at = 0
        for ref in (keep_near, keep_far, send_near, send_far):
            ref[:, cols] = answer[at : at + ref.shape[0]]
            at += ref.shape[0]


def expert_block(quarter, mine, near, cross, other, z, x, c, perm, wg, wu, wd, experts, before):
    far, wide = z.shape
    u = far // 3
    width = wide - EXTRA
    hidden = wd.shape[1]
    rows = 16 * u
    resident = pl.BlockSpec(memory_space=pltpu.VMEM)
    return pl.pallas_call(
        functools.partial(expert_kernel, experts, quarter, len(before)),
        in_specs=[pl.BlockSpec(memory_space=pltpu.SMEM)] + [resident] * (10 + len(before)),
        out_specs=[resident] * 5,
        out_shape=[jax.ShapeDtypeStruct((n * u, width), BF16) for n in (2, 6, 2, 6)]
        + [jax.ShapeDtypeStruct((8, 128), F32)],
        scratch_shapes=[
            pltpu.VMEM((rows, width), BF16),
            pltpu.VMEM((rows, hidden), BF16),
            pltpu.VMEM((rows, hidden), BF16),
        ],
        compiler_params=pltpu.CompilerParams(vmem_limit_bytes=14 * 1024 * 1024),
        cost_estimate=pl.CostEstimate(
            flops=2 * rows * width * hidden * 3,
            bytes_accessed=rows * width * 4,
            transcendentals=rows * hidden,
        ),
        name="expert_block",
    )(mine, near, cross, other, z, x, c, perm, wg, wu, wd, *before)


def dense(
    tokens,
    gate_scores,
    route_ids,
    gate_codes,
    up_codes,
    down_codes,
    gate_scale,
    up_scale,
    down_scale,
    gate_zero,
    up_zero,
    down_zero,
):
    experts = lax.axis_size("ep")
    n = tokens.shape[0]
    u = n // QUARTERS
    mine = lax.axis_index("ep").astype(jnp.int32).reshape(1)

    def swap(value, bits):
        return lax.ppermute(value, "ep", [(i, i ^ bits) for i in range(experts)])

    quarters = range(QUARTERS)
    rows, perm, mine = prepare(mine, tokens, gate_scores, route_ids, experts)

    half = n // 2
    cross = swap(rows, 2)
    first = [swap(rows[:half], 4 * k) for k in range(1, 4)]
    one = swap(rows[half:], 4)
    w_down, done_down = unpack(down_codes[0], down_scale[0], down_zero[0], 1792)
    w_gate, done_gate = unpack(gate_codes[0], gate_scale[0], gate_zero[0], 512)
    w_up, done_up = unpack(up_codes[0], up_scale[0], up_zero[0], 512)
    unpacked = [done_down, done_gate, done_up]

    z = [pack([(first[k], q * u, u) for k in range(3)], unpacked + [one]) for q in range(2)]
    onward = [pack([(rows, half + q * u, u), (one, q * u, u)], z) for q in range(2)]
    two = [swap(v, 8) for v in onward]
    other = swap(pack([(rows, 0, n), (cross, 0, n)], unpacked), 1)
    two_x = swap(pack([(cross, 3 * u, u)], unpacked), 8)
    x = [swap(v, 2) for v in z]
    done, near, far, sent = [], [], [], []

    def expert(q, ahead, before):
        both = pack([(z[q], 0, 3 * u), (x[q], 0, 3 * u)], done[-1:] + ahead)
        keep_near, keep_far, send_near, send_far, token = expert_block(
            q, mine, rows, cross, other, z[q], x[q], swap(both, 1), perm,
            w_gate, w_up, w_down, experts, before,
        )
        done.append(token)
        near.append((keep_near, send_near))
        far.append(keep_far)
        sent.append(send_far)

    def after_core(q, before):
        own, crossing = join([far[q]], [swap(sent[q], 1)], before)
        return own, crossing, swap(crossing, 2)

    z.append(pack([(one, 0, u), (two[0], 0, u), (two[0], u, u)]))
    expert(0, [z[2]], [])
    x.append(swap(z[2], 2))
    onward_x = pack([(cross, 3 * u, u), (two_x, 0, u)], done[-1:])
    one_x = swap(onward_x, 4)
    leaving_0, staying_0 = land(far[0], swap(sent[0], 1), 2, done[-1:])
    expert(1, [onward_x], [leaving_0, onward[1]])
    z.append(pack([(one, u, u), (two[1], 0, u), (two[1], u, u)], done[-1:]))
    x.append(pack([(one_x, 0, u), (two_x, 0, u), (one_x, u, u)], done[-1:]))
    own_1, crossing_1, crossed_1 = after_core(1, done[-1:])
    expert(2, [x[3], z[3]], [crossing_1])
    got_0 = swap(leaving_0, 4)
    passed_0 = pass_on(staying_0, got_0, done[-1:])
    leaving_1, staying_1 = land(own_1, crossed_1, 1, done[-1:])
    own_2, crossing_2, crossed_2 = after_core(2, done[-1:])
    expert(3, [passed_0, leaving_1], [crossing_2])
    got_1 = swap(leaving_1, 4)
    passed_1 = pass_on(staying_1, got_1, done[-1:])
    leaving_2, staying_2 = land(own_2, crossed_2, 1, done[-1:])
    sent[3] = pack([(sent[3], 0, 6 * u)], [passed_1, leaving_2])
    own_3, crossing_3, crossed_3 = after_core(3, done[-1:])
    leaving_3, staying_3 = land(own_3, crossed_3, 1)

    sends = [s for _, s in near]
    kept = [k for k, _ in near]
    send = pack([(s, 0, u) for s in sends] + [(s, u, u) for s in sends], done[-1:])
    keep = pack([(k, 0, u) for k in kept] + [(k, u, u) for k in kept], done[-1:])
    last_0 = swap(passed_0, 8)
    sum_0 = got_0[: 2 * u].astype(F32) + last_0.astype(F32)
    pair = keep.astype(F32) + swap(send, 1).astype(F32)
    away = jnp.concatenate([pair[n : n + u] + sum_0[u:], pair[n + u :]]).astype(BF16)
    over = [swap(away[:half], 2), swap(away[half:], 2)]
    got_2, got_3 = swap(leaving_2, 4), swap(leaving_3, 4)
    passed_2 = pass_on(staying_2, got_2, [crossing_3])
    passed_3 = pass_on(staying_3, got_3, [over[0]])
    sums = [sum_0[:u]]
    for got, passed in ((got_1, passed_1), (got_2, passed_2), (got_3, passed_3)):
        sums.append(got[:u].astype(F32) + swap(passed, 8).astype(F32))
    total = pair[:n] + jnp.concatenate(over).astype(F32) + jnp.concatenate(sums)
    return total.astype(BF16)


def solution(mesh):
    in_specs = (
        P(("grp", "ep"), "tp"),
        P(("grp", "ep"), None),
        P(("grp", "ep"), None),
        P("ep", None, "tp"),
        P("ep", None, "tp"),
        P("ep", None, "tp"),
        P("ep", None, "tp"),
        P("ep", None, "tp"),
        P("ep", None, "tp"),
        P("ep", None, "tp"),
        P("ep", None, "tp"),
        P("ep", None, "tp"),
    )
    out_specs = P(("grp", "ep"), "tp")
    experts = mesh.shape["ep"]
    few = mesh.shape["tp"] == 1 and experts == 16
    return jax.shard_map(
        dense if few else routed,
        mesh=mesh,
        in_specs=in_specs,
        out_specs=out_specs,
        check_vma=False,
    )
```
